32 devices in a mesh: tx: 16 (over z, y, core), ty: 2 (over x).
Axes of the slice: x: 2, y: 2, z: 4, core: 2. Of those that a mesh axis runs over, the one named last changes fastest.
Arguments:
- cells: bfloat16 [16, 2, 512, 512], P('tx', 'ty'), may hold values from -6 to 6
- halo_inputs: bfloat16 [16, 2, 256, 512], P('tx', 'ty'), may hold values from -6 to 6
- stale_halo: bfloat16 [16, 2, 1, 256, 512], P('tx', 'ty'), may hold values from -6 to 6
- stale_returned: bfloat16 [16, 2, 1, 256, 512], P('tx', 'ty'), may hold values from -3 to 3
- cotangent: bfloat16 [16, 2, 512, 512], P('tx', 'ty'), may hold values from -6 to 6
- expression: bfloat16 [16, 2, 512, 512], P('tx', 'ty'), may hold values from -6 to 6
- halo_expression: bfloat16 [16, 2, 256, 512], P('tx', 'ty'), may hold values from -6 to 6
- neighbours: int32 [16, 2, 16, 512], P('tx', 'ty'), may hold values from 0 to 767
- edge_mask: int32 [16, 2, 16, 512], P('tx', 'ty'), may hold values 0 or 1
- send_rows: int32 [16, 2, 8, 32], P('tx', 'ty'), may hold values from 0 to 511
- live_cells: int32 [16, 2], P('tx', 'ty'), may hold values from 256 to 512
- ligand_genes: int32 [1024], replicated, may hold values from 0 to 511
- receptor_genes: int32 [1024], replicated, may hold values from 0 to 511
- gate_weights: float32 [1024], replicated, may hold values from -0.1875 to 0.1875
- self_weights: bfloat16 [2, 512, 512], replicated, may hold values from -0.25 to 0.25
- neighbour_weights: bfloat16 [2, 512, 512], replicated, may hold values from -0.25 to 0.25
Outputs:
- fresh_halo: bfloat16 [16, 2, 1, 256, 512], P('tx', 'ty')
- returned_grads: bfloat16 [16, 2, 1, 256, 512], P('tx', 'ty')
- layer_updates: float32 [4, 512, 512], replicated
- gate_update: float32 [1024], replicated
The draws below stay inside these ranges and needn't reach their ends.
All inputs are finite; a program needn't handle non-finite values. No bound on the sum of `edge_mask` on one device may be relied on, other than what follows from the above.
Results may differ from the reference program's by a relative error of at most 0.0062.
Values may be sent and summed in bfloat16 or wider, within the bound.
A program may use at most 64 MiB of HBM per device.

```python
import jax
import jax.numpy as jnp
from jax import lax

WIDTH = 512
PAIRS = 1024
GENES = 512
DEGREE = 16
LAYERS = 2
CELLS = 512
BORDER = 32
HALO = 256
N_TX = 16
N_TY = 2


def plant(entries, stream_key, smallest, high):
    shape = entries.shape
    place = [jax.random.randint(jax.random.fold_in(stream_key, axis), (), 0, shape[axis]) for axis in range(len(shape))]
    entries = entries.at[tuple(place)].set(smallest)
    longest = shape.index(max(shape))
    place[longest] = (place[longest] + 1) % shape[longest]
    return entries.at[tuple(place)].set(high)


def level_of(rng, dims, shards, least, high):
    def one(axis_at, parts):
        steps = jax.random.uniform(jax.random.fold_in(jax.random.fold_in(rng, 6), axis_at), (parts,), jnp.float32, least / len(shards), high / len(shards))
        return jnp.repeat(jnp.exp(steps), dims[axis_at] // parts).reshape((-1,) + (1,) * (len(dims) - axis_at - 1))

    factor_of = one(*shards[0])
    for cut in shards[1:]:
        factor_of = factor_of * one(*cut)
    return factor_of


def normal_values(key, dims, deviation, reach, split=(), kind=jnp.bfloat16):
    result = jax.random.normal(key, dims, jnp.float32) * deviation
    if len(split) > 0:
        result = level_of(key, dims, split, -0.22, 0.18) * result
    return jnp.clip(result, min=-reach, max=reach).astype(kind)


def setup_inputs(seed: int = 0) -> dict:
    streams_of = jax.random.split(jax.random.key(seed), 17)
    cells = normal_values(streams_of[0], (N_TX, N_TY, CELLS, WIDTH), 1.0, 6.0, ((0, 16), (1, 2)))
    halo_inputs = normal_values(streams_of[1], (N_TX, N_TY, HALO, WIDTH), 1.0, 6.0, ((0, 16), (1, 2)))
    stale_halo = normal_values(streams_of[2], (N_TX, N_TY, LAYERS - 1, HALO, WIDTH), 1.0, 6.0, ((0, 16), (1, 2)))
    stale_returned = normal_values(streams_of[3], (N_TX, N_TY, LAYERS - 1, HALO, WIDTH), 0.5, 3.0, ((0, 16), (1, 2)))
    cotangent = normal_values(streams_of[4], (N_TX, N_TY, CELLS, WIDTH), 1.0, 6.0, ((0, 16), (1, 2)))
    expression = normal_values(streams_of[5], (N_TX, N_TY, CELLS, GENES), 1.0, 6.0, ((0, 16), (1, 2)))
    halo_expression = normal_values(streams_of[6], (N_TX, N_TY, HALO, GENES), 1.0, 6.0, ((0, 16), (1, 2)))
    neighbours = plant(jax.random.randint(streams_of[7], (N_TX, N_TY, DEGREE, CELLS), 0, CELLS + HALO), jax.random.fold_in(streams_of[7], 1), 0, (CELLS + HALO) - 1).astype(jnp.int32)
    edge_mask = plant((jax.random.randint(streams_of[8], (N_TX, N_TY, DEGREE, CELLS), 0, 4) < 3).astype(jnp.int32), jax.random.fold_in(streams_of[8], 1), 0, 1)
    send_rows = plant(jax.random.randint(streams_of[9], (N_TX, N_TY, 8, BORDER), 0, CELLS), jax.random.fold_in(streams_of[9], 1), 0, CELLS - 1).astype(jnp.int32)
    live_cells = plant(jax.random.randint(streams_of[10], (N_TX, N_TY), CELLS // 2, CELLS + 1), jax.random.fold_in(streams_of[10], 1), CELLS // 2, CELLS).astype(jnp.int32)
    ligand_genes = plant(jax.random.randint(streams_of[11], (PAIRS,), 0, GENES), jax.random.fold_in(streams_of[11], 1), 0, GENES - 1).astype(jnp.int32)
    receptor_genes = plant(jax.random.randint(streams_of[12], (PAIRS,), 0, GENES), jax.random.fold_in(streams_of[12], 1), 0, GENES - 1).astype(jnp.int32)
    gate_weights = normal_values(streams_of[13], (PAIRS,), PAIRS ** -0.5, 0.1875, (), jnp.float32)
    self_weights = normal_values(streams_of[14], (LAYERS, WIDTH, WIDTH), WIDTH ** -0.5, 0.25)
    neighbour_weights = normal_values(streams_of[15], (LAYERS, WIDTH, WIDTH), WIDTH ** -0.5, 0.25)
    return {"cells": cells, "halo_inputs": halo_inputs, "stale_halo": stale_halo, "stale_returned": stale_returned, "cotangent": cotangent, "expression": expression, "halo_expression": halo_expression, "neighbours": neighbours, "edge_mask": edge_mask, "send_rows": send_rows, "live_cells": live_cells, "ligand_genes": ligand_genes, "receptor_genes": receptor_genes, "gate_weights": gate_weights, "self_weights": self_weights, "neighbour_weights": neighbour_weights}


OFFSETS = ((-1, -1), (-1, 0), (-1, 1), (0, -1), (0, 1), (1, -1), (1, 0), (1, 1))

def silu_slope(pre_act):
    sigmoid_value = jax.nn.sigmoid(pre_act)
    return sigmoid_value * (1.0 + pre_act * (1.0 - sigmoid_value))

def tile_pass(tile_data, ligand_genes, receptor_genes, gate_weights, self_weights, neighbour_weights):
    own_state, halo_first, stale_rows, stale_back, upstream, genes_here, genes_halo, neighbour_ids, valid_edges, outgoing, live_count = tile_data
    cell_count = own_state.shape[0]
    model_width = own_state.shape[1]
    ligand = jnp.concatenate([genes_here, genes_halo], 0)[:, ligand_genes]
    receptor = genes_here[:, receptor_genes]
    scaled = receptor.astype(jnp.float32) * gate_weights[None, :]
    picked = ligand[neighbour_ids].astype(jnp.float32)
    edge_score = lax.optimization_barrier(jnp.sum(picked * scaled[None], axis=-1))
    gate_value = jax.nn.sigmoid(edge_score)
    weight = 0.25 * valid_edges.astype(jnp.float32) * gate_value
    states = [own_state]
    full_rows = []
    aggregates = []
    pre_acts = []
    for layer_id in range(LAYERS):
        halo_rows = halo_first if layer_id == 0 else stale_rows[layer_id - 1]
        joined = jnp.concatenate([states[layer_id], halo_rows], 0)
        gathered = joined[neighbour_ids].astype(jnp.float32)
        aggregate = lax.optimization_barrier(jnp.sum(weight[:, :, None] * gathered, axis=0)).astype(jnp.bfloat16)
        pre_act = jnp.dot(states[layer_id], self_weights[layer_id], preferred_element_type=jnp.float32)
        pre_act = pre_act + jnp.dot(aggregate, neighbour_weights[layer_id], preferred_element_type=jnp.float32)
        full_rows.append(joined)
        aggregates.append(aggregate)
        pre_acts.append(pre_act)
        if layer_id + 1 < LAYERS:
            states.append((states[layer_id].astype(jnp.float32) + jax.nn.silu(pre_act)).astype(jnp.bfloat16))
    live_rows = (jnp.arange(cell_count) < live_count)[:, None]
    grad_state = jnp.where(live_rows, upstream.astype(jnp.float32), jnp.float32(0.0))
    edge_grad = jnp.zeros(neighbour_ids.shape, jnp.float32)
    layer_grads = [None] * (2 * LAYERS)
    halo_grads = []
    for layer_id in range(LAYERS - 1, -1, -1):
        grad_pre = (grad_state * silu_slope(pre_acts[layer_id])).astype(jnp.bfloat16)
        layer_grads[2 * layer_id] = jnp.dot(states[layer_id].T, grad_pre, preferred_element_type=jnp.float32)
        layer_grads[2 * layer_id + 1] = jnp.dot(aggregates[layer_id].T, grad_pre, preferred_element_type=jnp.float32)
        grad_aggregate = jnp.dot(grad_pre, neighbour_weights[layer_id].T, preferred_element_type=jnp.float32).astype(jnp.bfloat16)
        wide_grad = grad_aggregate.astype(jnp.float32)
        gathered = full_rows[layer_id][neighbour_ids].astype(jnp.float32)
        edge_grad = edge_grad + lax.optimization_barrier(jnp.sum(gathered * wide_grad[None], axis=-1))
        if layer_id > 0:
            spread = (weight[:, :, None] * wide_grad[None]).reshape(-1, model_width)
            grad_full = jnp.zeros((full_rows[layer_id].shape[0], model_width), jnp.float32)
            grad_full = grad_full.at[neighbour_ids.reshape(-1)].add(spread)
            halo_grads.insert(0, grad_full[cell_count:].astype(jnp.bfloat16).reshape(8, -1, model_width))
            grad_state = grad_state + jnp.dot(grad_pre, self_weights[layer_id].T, preferred_element_type=jnp.float32)
            grad_state = grad_state + grad_full[:cell_count]
            grad_state = grad_state.at[outgoing.reshape(-1)].add(stale_back[layer_id - 1].astype(jnp.float32))
    grad_score = 0.25 * valid_edges.astype(jnp.float32) * edge_grad * gate_value * (1.0 - gate_value)
    gate_grad = lax.optimization_barrier(jnp.sum(lax.optimization_barrier(jnp.sum(grad_score[:, :, None] * picked, axis=0)) * receptor.astype(jnp.float32), axis=0))
    send_blocks = jnp.stack([states[layer_id][outgoing] for layer_id in range(1, LAYERS)])
    return (send_blocks, jnp.stack(halo_grads), jnp.stack(layer_grads), gate_grad)

def move_blocks(blocks, direction_sign):
    widths = ((1, 1), (1, 1)) + ((0, 0),) * (blocks.ndim - 2)
    padded = jnp.pad(blocks, widths)
    moved_list = []
    for direction, (delta_x, delta_y) in enumerate(OFFSETS):
        start_x = 1 - direction_sign * delta_x
        start_y = 1 - direction_sign * delta_y
        moved_list.append(padded[start_x:start_x + N_TX, start_y:start_y + N_TY, :, direction])
    return jnp.stack(moved_list, axis=3)

def reference(cells, halo_inputs, stale_halo, stale_returned, cotangent, expression, halo_expression, neighbours, edge_mask, send_rows, live_cells, ligand_genes, receptor_genes, gate_weights, self_weights, neighbour_weights):
    tile_count = N_TX * N_TY
    model_width = cells.shape[-1]
    per_tile = tuple((value.reshape((tile_count,) + value.shape[2:]) for value in (cells, halo_inputs, stale_halo, stale_returned, cotangent, expression, halo_expression, neighbours, edge_mask, send_rows, live_cells)))

    def tile_step(running, tile_data):
        send_blocks, halo_grads, layer_grads, gate_grad = tile_pass(tile_data, ligand_genes, receptor_genes, gate_weights, self_weights, neighbour_weights)
        return ((running[0] + layer_grads, running[1] + gate_grad), (send_blocks, halo_grads))
    initial = (jnp.zeros((2 * LAYERS, model_width, model_width), jnp.float32), jnp.zeros((PAIRS,), jnp.float32))
    (layer_sum, gate_sum), (send_all, halo_all) = lax.scan(tile_step, initial, per_tile)
    grid_shape = (N_TX, N_TY) + send_all.shape[1:]
    fresh_blocks = move_blocks(send_all.reshape(grid_shape), 1)
    returned_blocks = move_blocks(halo_all.reshape(grid_shape), -1)
    halo_shape = (N_TX, N_TY, LAYERS - 1, -1, model_width)
    square = jnp.sum(layer_sum * layer_sum) + jnp.sum(gate_sum * gate_sum)
    clip_factor = jnp.minimum(1.0, 2.0 * model_width / jnp.sqrt(square + 1e-06))
    return (fresh_blocks.reshape(halo_shape), returned_blocks.reshape(halo_shape), clip_factor * layer_sum, clip_factor * gate_sum)
```

```python
import functools

import jax
import jax.numpy as jnp
from jax import lax
from jax.experimental import pallas as pl
from jax.experimental.pallas import tpu as pltpu
from jax.sharding import PartitionSpec as P

OFFSETS = ((-1, -1), (-1, 0), (-1, 1), (0, -1), (0, 1), (1, -1), (1, 0), (1, 1))
F32 = jnp.float32
BF16 = jnp.bfloat16


def mm(a, b):
    return jnp.dot(a, b, preferred_element_type=F32)


def mm_nt(a, b):
    return lax.dot_general(a, b, (((1,), (1,)), ((), ())), preferred_element_type=F32)


def mm_tn(a, b):
    return lax.dot_general(a, b, (((0,), (0,)), ((), ())), preferred_element_type=F32)


def split(value):
    high = value.astype(BF16)
    return high, (value - high.astype(F32)).astype(BF16)


def sigmoid(value):
    return jax.nn.sigmoid(value)


def silu_slope(pre_act):
    gate = sigmoid(pre_act)
    return gate * (1.0 + pre_act * (1.0 - gate))


def count_edges(nbr_ref, mask_ref, count_ref):
    degree, cells = nbr_ref.shape[2:]
    rows = count_ref.shape[0]
    step = 32
    for lane in range(0, cells, 128):
        ids = []
        for k in range(degree):
            here = nbr_ref[0, 0, k : k + 1, lane : lane + 128]
            real = mask_ref[0, 0, k : k + 1, lane : lane + 128]
            ids.append(jnp.broadcast_to(jnp.where(real > 0, here, -1), (8, 128)))

        def body(chunk, carry):
            base = chunk * step
            for part in range(0, step, 8):
                row = lax.broadcasted_iota(jnp.int32, (8, 128), 0) + (base + part)
                total = jnp.zeros((8, 128), F32)
                for k in range(degree):
                    total = total + jnp.where(ids[k] == row, 1.0, 0.0)
                count_ref[pl.ds(pl.multiple_of(base + part, 8), 8), lane : lane + 128] = total
            return carry

        lax.fori_loop(0, rows // step, body, 0)


def one_hot(ids, rows):
    return lax.broadcasted_iota(jnp.int32, (rows, ids.shape[1]), 0) == ids


def flat_rows(send_ref):
    directions, border = send_ref.shape[2:]
    total = directions * border
    ids = send_ref[0, 0]
    spread = (
        lax.broadcasted_iota(jnp.int32, (border, total), 1) % border
        == lax.broadcasted_iota(jnp.int32, (border, total), 0)
    ).astype(BF16)
    high = mm((ids // 256).astype(F32).astype(BF16), spread)
    low = mm((ids % 256).astype(F32).astype(BF16), spread)
    wide = high * 256.0 + low
    mine = lax.broadcasted_iota(
        jnp.int32, (directions, total), 1
    ) // border == lax.broadcasted_iota(jnp.int32, (directions, total), 0)
    return jnp.sum(jnp.where(mine, wide, 0.0), axis=0, keepdims=True).astype(jnp.int32)


def tile_kernel(
    live_ref,
    cells_ref,
    halo_ref,
    stale_halo_ref,
    stale_ret_ref,
    cot_ref,
    expr_ref,
    halo_expr_ref,
    nbr_ref,
    mask_ref,
    send_ref,
    lig_ref,
    rec_ref,
    gate_ref,
    self_ref,
    neigh_ref,
    sent_ref,
    halo_grad_ref,
    grads_ref,
    gate_grad_ref,
    count_ref,
    adj_t_ref,
    adj_low_ref,
    slope_ref,
    prod_ref,
    genes_ref,
):
    layers = self_ref.shape[0]
    cells, width = cells_ref.shape[2:]
    halo = halo_ref.shape[2]
    joined_rows = cells + halo
    genes = expr_ref.shape[3]
    chunk = halo

    count_edges(nbr_ref, mask_ref, count_ref)

    receptor_hot = one_hot(rec_ref[...], genes)
    ligand_hot = one_hot(lig_ref[...], genes).astype(BF16)
    gate_high, gate_low = split(gate_ref[...])
    zero = jnp.zeros((), BF16)
    mix = mm_nt(jnp.where(receptor_hot, gate_high, zero), ligand_hot)
    mix = mix + mm_nt(jnp.where(receptor_hot, gate_low, zero), ligand_hot)
    mix_high, mix_low = split(mix)
    expr = expr_ref[0, 0]
    scaled_high, scaled_low = split(mm(expr, mix_high) + mm(expr, mix_low))
    genes_ref[0:cells, :] = expr
    genes_ref[cells:, :] = halo_expr_ref[0, 0]

    def score_chunk(step, carry):
        rows = pl.ds(pl.multiple_of(step * chunk, chunk), chunk)
        here = genes_ref[rows, :]
        score = mm_nt(here, scaled_high) + mm_nt(here, scaled_low)
        gate = sigmoid(score)
        base = 0.25 * count_ref[rows, :] * gate
        high, low = split(base)
        adj_t_ref[rows, :] = high
        adj_low_ref[rows, :] = low
        slope_ref[rows, :] = base * (1.0 - gate)
        return carry

    lax.fori_loop(0, joined_rows // chunk, score_chunk, 0)

    adjacency = adj_t_ref[...].T
    adjacency_low = adj_low_ref[...].T
    state = cells_ref[0, 0]
    states, full_rows, aggregates, pre_acts = [], [], [], []
    for layer in range(layers):
        halo_rows = halo_ref[0, 0] if layer == 0 else stale_halo_ref[0, 0, layer - 1]
        joined = jnp.concatenate([state, halo_rows], 0)
        aggregate = (mm(adjacency, joined) + mm(adjacency_low, joined)).astype(BF16)
        pre_act = mm(state, self_ref[layer]) + mm(aggregate, neigh_ref[layer])
        states.append(state)
        full_rows.append(joined)
        aggregates.append(aggregate)
        pre_acts.append(pre_act)
        if layer + 1 < layers:
            state = (state.astype(F32) + pre_act * sigmoid(pre_act)).astype(BF16)

    send_table = one_hot(flat_rows(send_ref), cells).astype(BF16)
    for layer in range(1, layers):
        sent_ref[layer - 1] = mm_tn(send_table, states[layer]).astype(BF16)

    live = lax.broadcasted_iota(jnp.int32, (cells, width), 0) < live_ref[0, 0]
    grad_state = jnp.where(live, cot_ref[0, 0].astype(F32), 0.0)
    grad_aggregates = [None] * layers
    for layer in range(layers - 1, -1, -1):
        grad_pre = (grad_state * silu_slope(pre_acts[layer])).astype(BF16)
        grads_ref[2 * layer] = mm_tn(states[layer], grad_pre)
        grads_ref[2 * layer + 1] = mm_tn(aggregates[layer], grad_pre)
        grad_aggregate = mm_nt(grad_pre, neigh_ref[layer]).astype(BF16)
        grad_aggregates[layer] = grad_aggregate
        if layer > 0:
            grad_full = mm(adj_t_ref[...], grad_aggregate)
            halo_grad_ref[layer - 1] = grad_full[cells:].astype(BF16)
            grad_state = (
                grad_state
                + mm_nt(grad_pre, self_ref[layer])
                + grad_full[:cells]
                + mm(send_table, stale_ret_ref[0, 0, layer - 1])
            )

    for start in range(0, joined_rows, chunk):
        inner = jnp.zeros((chunk, cells), F32)
        for layer in range(layers):
            inner = inner + mm_nt(
                full_rows[layer][start : start + chunk], grad_aggregates[layer]
            )
        score_grad = (slope_ref[start : start + chunk, :] * inner).astype(BF16)
        prod_ref[start : start + chunk, :] = mm(score_grad, expr).astype(BF16)
    pair_grads = mm_tn(genes_ref[...], prod_ref[...]).astype(BF16)
    picked = mm(pair_grads, receptor_hot.astype(BF16))
    gate_grad_ref[...] = jnp.sum(picked * ligand_hot.astype(F32), axis=0, keepdims=True)


def run_tile(*args):
    (
        cells,
        halo_inputs,
        stale_halo,
        stale_returned,
        cotangent,
        expression,
        halo_expression,
        neighbours,
        edge_mask,
        send_rows,
        live_cells,
        ligand_genes,
        receptor_genes,
        gate_weights,
        self_weights,
        neighbour_weights,
    ) = args
    layers, width, _ = self_weights.shape
    count, halo = cells.shape[2], halo_inputs.shape[2]
    genes, pairs = expression.shape[3], ligand_genes.shape[0]
    vmem = pl.BlockSpec(memory_space=pltpu.VMEM)
    smem = pl.BlockSpec(memory_space=pltpu.SMEM)
    return pl.pallas_call(
        tile_kernel,
        out_shape=(
            jax.ShapeDtypeStruct((layers - 1, halo, width), BF16),
            jax.ShapeDtypeStruct((layers - 1, halo, width), BF16),
            jax.ShapeDtypeStruct((2 * layers, width, width), F32),
            jax.ShapeDtypeStruct((1, pairs), F32),
        ),
        in_specs=[smem] + [vmem] * 15,
        out_specs=(vmem,) * 4,
        scratch_shapes=[
            pltpu.VMEM((count + halo, count), F32),
            pltpu.VMEM((count + halo, count), BF16),
            pltpu.VMEM((count + halo, count), BF16),
            pltpu.VMEM((count + halo, count), F32),
            pltpu.VMEM((count + halo, genes), BF16),
            pltpu.VMEM((count + halo, genes), BF16),
        ],
        compiler_params=pltpu.CompilerParams(vmem_limit_bytes=48 * 1024 * 1024),
        name="tile",
    )(
        live_cells,
        cells,
        halo_inputs,
        stale_halo,
        stale_returned,
        cotangent,
        expression,
        halo_expression,
        neighbours,
        edge_mask,
        send_rows,
        ligand_genes.reshape(1, -1),
        receptor_genes.reshape(1, -1),
        gate_weights.reshape(1, -1),
        self_weights,
        neighbour_weights,
    )


def shift(value, axis, steps):
    count = lax.axis_size(axis)
    first, last = max(0, -steps), min(count, count - steps)
    return lax.ppermute(value, axis, [(source, source + steps) for source in range(first, last)])


def route_blocks(blocks, block_axis):
    pieces = {}
    for direction, offset in enumerate(OFFSETS):
        pieces[offset] = lax.index_in_dim(blocks, direction, block_axis, keepdims=False)
    passed = {}
    for lead in (-1, 1):
        moved = shift(jnp.stack([pieces[lead, cross] for cross in (-1, 0, 1)]), "tx", lead)
        for position, cross in enumerate((-1, 0, 1)):
            passed[lead, cross] = moved[position]
    arrived = {(-1, 0): passed[-1, 0], (1, 0): passed[1, 0]}
    for cross in (-1, 1):
        payload = jnp.stack([pieces[0, cross], passed[-1, cross], passed[1, cross]])
        moved = shift(payload, "ty", cross)
        arrived[0, cross] = moved[0]
        arrived[-1, cross] = moved[1]
        arrived[1, cross] = moved[2]
    return jnp.stack([arrived[offset] for offset in OFFSETS], block_axis)


def on_device(*args):
    self_weights = args[14]
    layers, width, _ = self_weights.shape
    sent, halo_grads, layer_grads, gate_grad = run_tile(*args)
    sent_blocks = sent.reshape(layers - 1, 8, -1, width)
    grad_blocks = jnp.flip(halo_grads.reshape(layers - 1, 8, -1, width), 1)
    combined = route_blocks(jnp.stack([sent_blocks, grad_blocks]), 2)
    returned = jnp.flip(combined[1], 1)
    layer_sum, gate_sum = lax.psum((layer_grads, gate_grad[0]), ("tx", "ty"))
    square = jnp.sum(layer_sum * layer_sum) + jnp.sum(gate_sum * gate_sum)
    clip = jnp.minimum(1.0, 2.0 * width / jnp.sqrt(square + 1e-06))
    halo_shape = (1, 1, layers - 1, -1, width)
    return (
        combined[0].reshape(halo_shape),
        returned.reshape(halo_shape),
        clip * layer_sum,
        clip * gate_sum,
    )


def solution(mesh):
    tile = P("tx", "ty")
    return jax.shard_map(
        on_device,
        mesh=mesh,
        in_specs=(tile,) * 11 + (P(),) * 5,
        out_specs=(tile, tile, P(), P()),
        check_vma=False,
    )
```

```python
import functools

import jax
import jax.numpy as jnp
from jax import lax
from jax.experimental import pallas as pl
from jax.experimental.pallas import tpu as pltpu
from jax.sharding import PartitionSpec as P

OFFSETS = ((-1, -1), (-1, 0), (-1, 1), (0, -1), (0, 1), (1, -1), (1, 0), (1, 1))
F32 = jnp.float32
BF16 = jnp.bfloat16
LANES = 128


def mm(a, b):
    return jnp.dot(a, b, preferred_element_type=F32)


def mm_nt(a, b):
    return lax.dot_general(a, b, (((1,), (1,)), ((), ())), preferred_element_type=F32)


def mm_tn(a, b):
    return lax.dot_general(a, b, (((0,), (0,)), ((), ())), preferred_element_type=F32)


def split(value):
    high = value.astype(BF16)
    return high, (value - high.astype(F32)).astype(BF16)


def sigmoid(value):
    return jax.nn.sigmoid(value)


def silu_slope(pre_act):
    gate = sigmoid(pre_act)
    return gate * (1.0 + pre_act * (1.0 - gate))


def count_edges(nbr_ref, mask_ref, count_ref):
    degree, cells = nbr_ref.shape[2:]
    rows = count_ref.shape[0]
    step = 32
    for lane in range(0, cells, 128):
        ids = []
        for k in range(degree):
            here = nbr_ref[0, 0, k : k + 1, lane : lane + 128]
            real = mask_ref[0, 0, k : k + 1, lane : lane + 128]
            ids.append(jnp.broadcast_to(jnp.where(real > 0, here, -1), (8, 128)))

        def body(chunk, carry):
            base = chunk * step
            for part in range(0, step, 8):
                row = lax.broadcasted_iota(jnp.int32, (8, 128), 0) + (base + part)
                total = jnp.zeros((8, 128), F32)
                for k in range(degree):
                    total = total + jnp.where(ids[k] == row, 1.0, 0.0)
                count_ref[pl.ds(pl.multiple_of(base + part, 8), 8), lane : lane + 128] = total
            return carry

        lax.fori_loop(0, rows // step, body, 0)


def one_hot(ids, rows):
    return lax.broadcasted_iota(jnp.int32, (rows, ids.shape[1]), 0) == ids


def flat_rows(send_ref):
    directions, border = send_ref.shape[2:]
    total = directions * border
    ids = send_ref[0, 0]
    spread = (
        lax.broadcasted_iota(jnp.int32, (border, total), 1) % border
        == lax.broadcasted_iota(jnp.int32, (border, total), 0)
    ).astype(BF16)
    high = mm((ids // 256).astype(F32).astype(BF16), spread)
    low = mm((ids % 256).astype(F32).astype(BF16), spread)
    wide = high * 256.0 + low
    mine = lax.broadcasted_iota(
        jnp.int32, (directions, total), 1
    ) // border == lax.broadcasted_iota(jnp.int32, (directions, total), 0)
    return jnp.sum(jnp.where(mine, wide, 0.0), axis=0, keepdims=True).astype(jnp.int32)


def bits_of(size):
    assert size & (size - 1) == 0
    return size.bit_length() - 1


def stream_orders(tx_size, ty_size):
    tx_bits = [("tx", bit) for bit in range(bits_of(tx_size))]
    ty_bits = [("ty", bit) for bit in range(bits_of(ty_size))]
    first, second, rest = tx_bits[:1], tx_bits[1:2], tx_bits[2:]
    return (
        first + ty_bits + second + rest,
        first + second + rest[:1] + ty_bits + rest[1:],
        first + rest[:1] + ty_bits + second + rest[1:],
    )


def stream_ranges(rows, devices):
    unit = 16 * devices
    units = rows // unit
    assert units * unit == rows and units > 0
    used = min(3, units)
    ranges, start = [], 0
    for stream in range(used):
        size = (units // used + (1 if stream < units % used else 0)) * unit
        ranges.append((start, size))
        start += size
    return ranges


class Exchange:
    def __init__(
        self,
        sizes,
        grads_ref,
        sum_ref,
        sent_ref,
        halo_grad_ref,
        fresh_ref,
        returned_ref,
        work_ref,
        landing_ref,
        gate_acc,
        gate_land,
        square_acc,
        square_land,
        send_sems,
        recv_sems,
        small_send,
        small_recv,
        halo_send,
        halo_recv,
    ):
        self.sizes = sizes
        self.me = {"tx": lax.axis_index("tx"), "ty": lax.axis_index("ty")}
        self.grads, self.sum, self.work, self.landing = grads_ref, sum_ref, work_ref, landing_ref
        self.halo = ((sent_ref, fresh_ref, 1), (halo_grad_ref, returned_ref, -1))
        self.small = ((gate_acc, gate_land), (square_acc, square_land))
        self.sems = (send_sems, recv_sems)
        self.small_sems = (small_send, small_recv)
        self.halo_sems = (halo_send, halo_recv)
        self.orders = stream_orders(*sizes)
        self.steps = len(self.orders[0])
        self.landed = 0
        self.streams = []
        self.smalls = []
        self.sending = []
        self.exchanges = []
        self.squares = None

    def bit(self, where):
        axis, bit = where
        return (self.me[axis] // (1 << bit)) % 2

    def partner(self, where):
        axis, bit = where
        return {axis: self.me[axis] + (1 - 2 * self.bit(where)) * (1 << bit)}

    def inside(self, delta_x, delta_y):
        x, y = self.me["tx"] + delta_x, self.me["ty"] + delta_y
        return (x >= 0) & (x < self.sizes[0]) & (y >= 0) & (y < self.sizes[1])

    def offset(self, delta_x, delta_y):
        return {"tx": self.me["tx"] + delta_x, "ty": self.me["ty"] + delta_y}

    def announce(self):
        barrier = pltpu.get_barrier_semaphore()

        def greet(device):
            pl.semaphore_signal(
                barrier, inc=1, device_id=device, device_id_type=pl.DeviceIdType.MESH
            )

        for where in self.orders[0]:
            greet(self.partner(where))
        for offset in OFFSETS:
            pl.when(self.inside(*offset))(lambda offset=offset: greet(self.offset(*offset)))

    def meet(self):
        barrier = pltpu.get_barrier_semaphore()
        peers = self.steps
        for offset in OFFSETS:
            peers = peers + self.inside(*offset).astype(jnp.int32)
        pl.semaphore_wait(barrier, peers)

    def copy(self, source, target, send, recv, device):
        return pltpu.make_async_remote_copy(
            src_ref=source,
            dst_ref=target,
            send_sem=send,
            recv_sem=recv,
            device_id=device,
            device_id_type=pl.DeviceIdType.MESH,
        )

    def begin(self, copy):
        copy.start()
        self.sending.append(copy)
        return copy

    def send_halo(self, kind):
        source, target, sign = self.halo[kind]
        depth, rows, width = source.shape
        border = rows // 8
        for direction, (delta_x, delta_y) in enumerate(OFFSETS):
            part = pl.ds(direction * border, border)
            goes = self.inside(sign * delta_x, sign * delta_y)
            comes = self.inside(-sign * delta_x, -sign * delta_y)
            copy = self.copy(
                source.at[:, part, :],
                target.at[:, part, :],
                self.halo_sems[0].at[kind, direction],
                self.halo_sems[1].at[kind, direction],
                self.offset(sign * delta_x, sign * delta_y),
            )

            @pl.when(goes)
            def _():
                copy.start()

            @pl.when(jnp.logical_not(comes))
            def _():
                target[:, part, :] = jnp.zeros((depth, border, width), BF16)

            self.exchanges.append((copy, goes, comes))

    def open(self, layer, layers):
        rows = self.grads.shape[0] // layers
        for number, (start, size) in enumerate(
            stream_ranges(rows, self.sizes[0] * self.sizes[1])
        ):
            stream = dict(
                slot=len(self.streams),
                order=self.orders[number],
                low=layer * rows + start,
                span=size,
                step=0,
                past=[],
            )
            self.streams.append(stream)
            self.reduce_start(stream)

    def block(self, start, size):
        return pl.ds(pl.multiple_of(start, 16), size)

    def reduce_start(self, stream):
        step, half = stream["step"], stream["span"] // 2
        where = stream["order"][step]
        bit = self.bit(where)
        stream["past"].append((stream["low"], stream["span"]))
        give = stream["low"] + (1 - bit) * half
        stream["target"] = self.landing.at[pl.ds(self.landed, half), :]
        stream["copy"] = self.begin(
            self.copy(
                self.work.at[self.block(give, half), :],
                stream["target"],
                self.sems[0].at[stream["slot"], step],
                self.sems[1].at[stream["slot"], step],
                self.partner(where),
            )
        )
        stream["low"], stream["span"] = stream["low"] + bit * half, half
        self.landed += half

    def gather_start(self, stream):
        step = stream["step"]
        where = stream["order"][2 * self.steps - 1 - step]
        here = self.block(stream["low"], stream["span"])
        stream["copy"] = self.begin(
            self.copy(
                self.sum.at[here, :],
                self.sum.at[here, :],
                self.sems[0].at[stream["slot"], step],
                self.sems[1].at[stream["slot"], step],
                self.partner(where),
            )
        )
        stream["low"], stream["span"] = stream["past"].pop()

    def advance_one(self, stream):
        stream["copy"].wait_recv()
        step = stream["step"]
        stream["step"] = step + 1
        if step < self.steps:
            here = self.block(stream["low"], stream["span"])
            total = self.grads[here, :] + stream["target"][...].astype(F32)
            if step + 1 < self.steps:
                self.grads[here, :] = total
                self.work[here, :] = total.astype(BF16)
                self.reduce_start(stream)
            else:
                self.sum[here, :] = total.astype(BF16)
                squares = jnp.sum((total * total).reshape(-1, 8, LANES), axis=0)
                self.squares = squares if self.squares is None else self.squares + squares
                self.gather_start(stream)
        elif step + 1 < 2 * self.steps:
            self.gather_start(stream)

    def advance(self):
        for stream in self.streams:
            if stream["step"] < 2 * self.steps:
                self.advance_one(stream)

    def small_start(self, small):
        step, kind = small["step"], small["kind"]
        acc, land = self.small[kind]
        small["copy"] = self.begin(
            self.copy(
                acc.at[step],
                land.at[step],
                self.small_sems[0].at[kind, step],
                self.small_sems[1].at[kind, step],
                self.partner(self.orders[0][step]),
            )
        )

    def open_small(self, kind):
        small = dict(kind=kind, step=0)
        self.small_start(small)
        return small

    def advance_small(self, small):
        step = small["step"]
        acc, land = self.small[small["kind"]]
        small["copy"].wait_recv()
        acc[step + 1] = acc[step] + land[step]
        small["step"] = step + 1
        if step + 1 < self.steps:
            self.small_start(small)

    def open_gate(self, gate_grad):
        acc = self.small[0][0]
        for row in range(acc.shape[1]):
            acc[0, row : row + 1, :] = gate_grad[:, row * LANES : (row + 1) * LANES]
        self.smalls.append(self.open_small(0))

    def finish(self):
        steps = self.steps
        while any(stream["step"] < 2 * steps for stream in self.streams) or any(
            small["step"] < steps for small in self.smalls
        ):
            self.advance()
            for small in self.smalls:
                if small["step"] < steps:
                    self.advance_small(small)
            if len(self.smalls) == 1 and all(stream["step"] >= steps for stream in self.streams):
                self.small[1][0][0] = self.squares
                self.smalls.append(self.open_small(1))
        for copy, goes, comes in self.exchanges:
            pl.when(comes)(copy.wait_recv)
            pl.when(goes)(copy.wait_send)
        for copy in self.sending:
            copy.wait_send()
        gate = self.small[0][0][steps]
        square = jnp.sum(self.small[1][0][steps], keepdims=True)
        return gate, square + jnp.sum(gate * gate, keepdims=True)


LOADED = (
    "nbr",
    "mask",
    "expr",
    "halo_expr",
    "cells",
    "halo",
    "self",
    "neigh",
    "stale_halo",
    "send",
    "cot",
    "stale_ret",
)


def step_kernel(sizes, *refs):
    total = len(LOADED)
    live_ref, lig_ref, rec_ref, gate_ref = refs[:4]
    far = refs[4 : 4 + total]
    fresh_ref, returned_ref, sum_ref, gate_out_ref, clip_ref = refs[4 + total : 9 + total]
    near = refs[9 + total : 9 + 2 * total]
    (
        count_ref,
        adj_t_ref,
        adj_low_ref,
        slope_ref,
        prod_ref,
        genes_ref,
        sent_ref,
        halo_grad_ref,
        grads_ref,
        sems,
    ) = refs[9 + 2 * total : 19 + 2 * total]
    link = Exchange(
        sizes,
        grads_ref,
        sum_ref,
        sent_ref,
        halo_grad_ref,
        fresh_ref,
        returned_ref,
        *refs[19 + 2 * total :],
    )
    link.announce()
    copies = {}
    for position, name in enumerate(LOADED):
        copies[name] = pltpu.make_async_copy(far[position], near[position], sems.at[position])
        copies[name].start()
    place = dict(zip(LOADED, near))

    def arrived(name):
        copies[name].wait()
        return place[name]

    layers = place["self"].shape[0]
    cells, width = place["cells"].shape[2:]
    halo = place["halo"].shape[2]
    joined_rows = cells + halo
    genes = place["expr"].shape[3]
    chunk = halo

    nbr_ref, mask_ref = arrived("nbr"), arrived("mask")
    count_edges(nbr_ref, mask_ref, count_ref)

    receptor_hot = one_hot(rec_ref[...], genes)
    ligand_hot = one_hot(lig_ref[...], genes).astype(BF16)
    gate_high, gate_low = split(gate_ref[...])
    zero = jnp.zeros((), BF16)
    mix = mm_nt(jnp.where(receptor_hot, gate_high, zero), ligand_hot)
    mix = mix + mm_nt(jnp.where(receptor_hot, gate_low, zero), ligand_hot)
    mix_high, mix_low = split(mix)
    expr = arrived("expr")[0, 0]
    scaled_high, scaled_low = split(mm(expr, mix_high) + mm(expr, mix_low))
    genes_ref[0:cells, :] = expr
    genes_ref[cells:, :] = arrived("halo_expr")[0, 0]

    def score_chunk(step, carry):
        rows = pl.ds(pl.multiple_of(step * chunk, chunk), chunk)
        here = genes_ref[rows, :]
        score = mm_nt(here, scaled_high) + mm_nt(here, scaled_low)
        gate = sigmoid(score)
        base = 0.25 * count_ref[rows, :] * gate
        high, low = split(base)
        adj_t_ref[rows, :] = high
        adj_low_ref[rows, :] = low
        slope_ref[rows, :] = base * (1.0 - gate)
        return carry

    lax.fori_loop(0, joined_rows // chunk, score_chunk, 0)

    adjacency = adj_t_ref[...].T
    adjacency_low = adj_low_ref[...].T
    state = arrived("cells")[0, 0]
    halo_ref, self_ref, neigh_ref = arrived("halo"), arrived("self"), arrived("neigh")
    stale_halo_ref = arrived("stale_halo")
    states, full_rows, aggregates, pre_acts = [], [], [], []
    for layer in range(layers):
        halo_rows = halo_ref[0, 0] if layer == 0 else stale_halo_ref[0, 0, layer - 1]
        joined = jnp.concatenate([state, halo_rows], 0)
        aggregate = (mm(adjacency, joined) + mm(adjacency_low, joined)).astype(BF16)
        pre_act = mm(state, self_ref[layer]) + mm(aggregate, neigh_ref[layer])
        states.append(state)
        full_rows.append(joined)
        aggregates.append(aggregate)
        pre_acts.append(pre_act)
        if layer + 1 < layers:
            state = (state.astype(F32) + pre_act * sigmoid(pre_act)).astype(BF16)

    send_table = one_hot(flat_rows(arrived("send")), cells).astype(BF16)
    for layer in range(1, layers):
        sent_ref[layer - 1] = mm_tn(send_table, states[layer]).astype(BF16)
    link.meet()
    link.send_halo(0)

    cot_ref, stale_ret_ref = arrived("cot"), arrived("stale_ret")
    live = lax.broadcasted_iota(jnp.int32, (cells, width), 0) < live_ref[0, 0]
    grad_state = jnp.where(live, cot_ref[0, 0].astype(F32), 0.0)
    grad_aggregates = [None] * layers
    for layer in range(layers - 1, -1, -1):
        grad_pre = (grad_state * silu_slope(pre_acts[layer])).astype(BF16)
        for position, left in enumerate((states[layer], aggregates[layer])):
            product = mm_tn(left, grad_pre)
            for lane in range(0, width, LANES):
                start = (2 * layer + position) * width * width // LANES + lane // LANES * width
                grads_ref[start : start + width, :] = product[:, lane : lane + LANES]
                link.work[start : start + width, :] = product[:, lane : lane + LANES].astype(BF16)
        link.open(layer, layers)
        grad_aggregate = mm_nt(grad_pre, neigh_ref[layer]).astype(BF16)
        grad_aggregates[layer] = grad_aggregate
        if layer > 0:
            grad_full = mm(adj_t_ref[...], grad_aggregate)
            halo_grad_ref[layer - 1] = grad_full[cells:].astype(BF16)
            grad_state = (
                grad_state
                + mm_nt(grad_pre, self_ref[layer])
                + grad_full[:cells]
                + mm(send_table, stale_ret_ref[0, 0, layer - 1])
            )
            link.advance()
    link.send_halo(1)

    for start in range(0, joined_rows, chunk):
        inner = jnp.zeros((chunk, cells), F32)
        for layer in range(layers):
            inner = inner + mm_nt(
                full_rows[layer][start : start + chunk], grad_aggregates[layer]
            )
        score_grad = (slope_ref[start : start + chunk, :] * inner).astype(BF16)
        prod_ref[start : start + chunk, :] = mm(score_grad, expr).astype(BF16)
        link.advance()
    pair_grads = mm_tn(genes_ref[...], prod_ref[...]).astype(BF16)
    link.advance()
    picked = mm(pair_grads, receptor_hot.astype(BF16))
    gate_grad = jnp.sum(picked * ligand_hot.astype(F32), axis=0, keepdims=True)
    link.open_gate(gate_grad)
    gate_sum, square = link.finish()
    clip = jnp.minimum(1.0, 2.0 * width / jnp.sqrt(square + 1e-06))
    clip_ref[...] = jnp.broadcast_to(clip, clip_ref.shape)
    gate_out_ref[...] = gate_sum * clip


def run_step(sizes, *args):
    (
        cells,
        halo_inputs,
        stale_halo,
        stale_returned,
        cotangent,
        expression,
        halo_expression,
        neighbours,
        edge_mask,
        send_rows,
        live_cells,
        ligand_genes,
        receptor_genes,
        gate_weights,
        self_weights,
        neighbour_weights,
    ) = args
    layers, width, _ = self_weights.shape
    count, halo = cells.shape[2], halo_inputs.shape[2]
    genes, pairs = expression.shape[3], ligand_genes.shape[0]
    vmem = pl.BlockSpec(memory_space=pltpu.VMEM)
    smem = pl.BlockSpec(memory_space=pltpu.SMEM)
    hbm = pl.BlockSpec(memory_space=pltpu.HBM)
    named = dict(
        nbr=neighbours,
        mask=edge_mask,
        expr=expression,
        halo_expr=halo_expression,
        cells=cells,
        halo=halo_inputs,
        self=self_weights,
        neigh=neighbour_weights,
        stale_halo=stale_halo,
        send=send_rows,
        cot=cotangent,
        stale_ret=stale_returned,
    )
    loaded = [named[name] for name in LOADED]
    rows = 2 * layers * width * width // LANES
    steps = bits_of(sizes[0] * sizes[1])
    streams = layers * len(stream_ranges(rows // layers, sizes[0] * sizes[1]))
    edges = (layers - 1, halo, width)
    gate_tile = (pairs // LANES, LANES)
    return pl.pallas_call(
        functools.partial(step_kernel, sizes),
        out_shape=(
            jax.ShapeDtypeStruct(edges, BF16),
            jax.ShapeDtypeStruct(edges, BF16),
            jax.ShapeDtypeStruct((rows, LANES), BF16),
            jax.ShapeDtypeStruct(gate_tile, F32),
            jax.ShapeDtypeStruct((8, LANES), F32),
        ),
        in_specs=[smem] + [vmem] * 3 + [hbm] * len(loaded),
        out_specs=(vmem,) * 5,
        scratch_shapes=[pltpu.VMEM(value.shape, value.dtype) for value in loaded]
        + [
            pltpu.VMEM((count + halo, count), F32),
            pltpu.VMEM((count + halo, count), BF16),
            pltpu.VMEM((count + halo, count), BF16),
            pltpu.VMEM((count + halo, count), F32),
            pltpu.VMEM((count + halo, genes), BF16),
            pltpu.VMEM((count + halo, genes), BF16),
            pltpu.VMEM(edges, BF16),
            pltpu.VMEM(edges, BF16),
            pltpu.VMEM((rows, LANES), F32),
            pltpu.SemaphoreType.DMA((len(loaded),)),
            pltpu.VMEM((rows, LANES), BF16),
            pltpu.VMEM((rows, LANES), BF16),
            pltpu.VMEM((steps + 1,) + gate_tile, F32),
            pltpu.VMEM((steps + 1,) + gate_tile, F32),
            pltpu.VMEM((steps + 1, 8, LANES), F32),
            pltpu.VMEM((steps + 1, 8, LANES), F32),
            pltpu.SemaphoreType.DMA((streams, 2 * steps)),
            pltpu.SemaphoreType.DMA((streams, 2 * steps)),
            pltpu.SemaphoreType.DMA((2, steps)),
            pltpu.SemaphoreType.DMA((2, steps)),
            pltpu.SemaphoreType.DMA((2, 8)),
            pltpu.SemaphoreType.DMA((2, 8)),
        ],
        compiler_params=pltpu.CompilerParams(
            collective_id=0, has_side_effects=True, vmem_limit_bytes=58 * 1024 * 1024
        ),
        name="step",
    )(
        live_cells,
        ligand_genes.reshape(1, -1),
        receptor_genes.reshape(1, -1),
        gate_weights.reshape(1, -1),
        *loaded,
    )


def on_device(sizes, *args):
    self_weights = args[14]
    layers, width, _ = self_weights.shape
    fresh, returned, layer_sum, gate, clip = run_step(sizes, *args)
    halo_shape = (1, 1) + fresh.shape
    blocks = layer_sum.reshape(2 * layers, width // LANES, width, LANES)
    blocks = blocks.transpose(0, 2, 1, 3).reshape(2 * layers, width, width)
    return (
        fresh.reshape(halo_shape),
        returned.reshape(halo_shape),
        clip[0, 0] * blocks.astype(F32),
        gate.reshape(-1),
    )


def solution(mesh):
    tile = P("tx", "ty")
    sizes = (mesh.shape["tx"], mesh.shape["ty"])
    return jax.shard_map(
        functools.partial(on_device, sizes),
        mesh=mesh,
        in_specs=(tile,) * 11 + (P(),) * 5,
        out_specs=(tile, tile, P(), P()),
        check_vma=False,
    )
```

```python
import functools

import jax
import jax.numpy as jnp
from jax import lax
from jax.experimental import pallas as pl
from jax.experimental.pallas import tpu as pltpu
from jax.sharding import PartitionSpec as P

OFFSETS = ((-1, -1), (-1, 0), (-1, 1), (0, -1), (0, 1), (1, -1), (1, 0), (1, 1))
F32 = jnp.float32
BF16 = jnp.bfloat16
LANES = 128


def mm(a, b):
    return jnp.dot(a, b, preferred_element_type=F32)


def mm_nt(a, b):
    return lax.dot_general(a, b, (((1,), (1,)), ((), ())), preferred_element_type=F32)


def mm_tn(a, b):
    return lax.dot_general(a, b, (((0,), (0,)), ((), ())), preferred_element_type=F32)


def split(value):
    high = value.astype(BF16)
    return high, (value - high.astype(F32)).astype(BF16)


def sigmoid(value):
    return jax.nn.sigmoid(value)


def silu_slope(pre_act):
    gate = sigmoid(pre_act)
    return gate * (1.0 + pre_act * (1.0 - gate))


def count_edges(nbr_ref, mask_ref, count_ref):
    degree, cells = nbr_ref.shape[2:]
    rows = count_ref.shape[0]
    step, group = 64, 256
    for lane in range(0, cells, 128):
        for first in range(0, rows, group):
            ids = []
            for k in range(degree):
                here = nbr_ref[0, 0, k : k + 1, lane : lane + 128] - first
                real = mask_ref[0, 0, k : k + 1, lane : lane + 128]
                near = jnp.where(real > 0, here, -1).astype(F32)
                ids.append(jnp.broadcast_to(near, (16, 128)).astype(BF16))

            def body(chunk, carry):
                for part in range(0, step, 16):
                    base = chunk * step + part
                    row = lax.broadcasted_iota(jnp.int32, (16, 128), 0) + base
                    row = row.astype(F32).astype(BF16)
                    total = jnp.zeros((16, 128), BF16)
                    one = jnp.ones((16, 128), BF16)
                    for k in range(degree):
                        total = total + jnp.where(ids[k] == row, one, jnp.zeros_like(one))
                    start = pl.multiple_of(first + base, 16)
                    count_ref[pl.ds(start, 16), lane : lane + 128] = total
                return carry

            lax.fori_loop(0, min(group, rows - first) // step, body, 0)


def one_hot(ids, rows):
    return lax.broadcasted_iota(jnp.int32, (rows, ids.shape[1]), 0) == ids


def flat_rows(send_ref):
    directions, border = send_ref.shape[2:]
    total = directions * border
    ids = send_ref[0, 0]
    spread = (
        lax.broadcasted_iota(jnp.int32, (border, total), 1) % border
        == lax.broadcasted_iota(jnp.int32, (border, total), 0)
    ).astype(BF16)
    high = mm((ids // 256).astype(F32).astype(BF16), spread)
    low = mm((ids % 256).astype(F32).astype(BF16), spread)
    wide = high * 256.0 + low
    mine = lax.broadcasted_iota(
        jnp.int32, (directions, total), 1
    ) // border == lax.broadcasted_iota(jnp.int32, (directions, total), 0)
    return jnp.sum(jnp.where(mine, wide, 0.0), axis=0, keepdims=True).astype(jnp.int32)


def bits_of(size):
    assert size & (size - 1) == 0
    return size.bit_length() - 1


def stream_orders(tx_size, ty_size):
    tx_bits = [("tx", bit) for bit in range(bits_of(tx_size))]
    ty_bits = [("ty", bit) for bit in range(bits_of(ty_size))]
    first, second, rest = tx_bits[:1], tx_bits[1:2], tx_bits[2:]
    return (
        first + ty_bits + second + rest,
        first + second + rest[:1] + ty_bits + rest[1:],
        first + rest[:1] + ty_bits + second + rest[1:],
    )


def stream_ranges(rows, devices):
    unit = 16 * devices
    units = rows // unit
    assert units * unit == rows and units > 0
    used = min(3, units)
    ranges, start = [], 0
    for stream in range(used):
        size = (units // used + (1 if stream < units % used else 0)) * unit
        ranges.append((start, size))
        start += size
    return ranges


class Exchange:
    def __init__(
        self,
        sizes,
        grads_ref,
        sum_ref,
        sent_ref,
        halo_grad_ref,
        fresh_ref,
        returned_ref,
        work_ref,
        landing_ref,
        gate_acc,
        gate_land,
        square_acc,
        square_land,
        send_sems,
        recv_sems,
        small_send,
        small_recv,
        halo_send,
        halo_recv,
    ):
        self.sizes = sizes
        self.me = {"tx": lax.axis_index("tx"), "ty": lax.axis_index("ty")}
        self.grads, self.sum, self.work, self.landing = grads_ref, sum_ref, work_ref, landing_ref
        self.halo = ((sent_ref, fresh_ref, 1), (halo_grad_ref, returned_ref, -1))
        self.small = ((gate_acc, gate_land), (square_acc, square_land))
        self.sems = (send_sems, recv_sems)
        self.small_sems = (small_send, small_recv)
        self.halo_sems = (halo_send, halo_recv)
        self.orders = stream_orders(*sizes)
        self.steps = len(self.orders[0])
        self.landed = 0
        self.streams = []
        self.smalls = []
        self.sending = []
        self.exchanges = []
        self.squares = None

    def bit(self, where):
        axis, bit = where
        return (self.me[axis] // (1 << bit)) % 2

    def partner(self, where):
        axis, bit = where
        return {axis: self.me[axis] + (1 - 2 * self.bit(where)) * (1 << bit)}

    def inside(self, delta_x, delta_y):
        x, y = self.me["tx"] + delta_x, self.me["ty"] + delta_y
        return (x >= 0) & (x < self.sizes[0]) & (y >= 0) & (y < self.sizes[1])

    def offset(self, delta_x, delta_y):
        return {"tx": self.me["tx"] + delta_x, "ty": self.me["ty"] + delta_y}

    def announce(self):
        barrier = pltpu.get_barrier_semaphore()

        def greet(device):
            pl.semaphore_signal(
                barrier, inc=1, device_id=device, device_id_type=pl.DeviceIdType.MESH
            )

        for where in self.orders[0]:
            greet(self.partner(where))
        for offset in OFFSETS:
            pl.when(self.inside(*offset))(lambda offset=offset: greet(self.offset(*offset)))

    def meet(self):
        barrier = pltpu.get_barrier_semaphore()
        peers = self.steps
        for offset in OFFSETS:
            peers = peers + self.inside(*offset).astype(jnp.int32)
        pl.semaphore_wait(barrier, peers)

    def copy(self, source, target, send, recv, device):
        return pltpu.make_async_remote_copy(
            src_ref=source,
            dst_ref=target,
            send_sem=send,
            recv_sem=recv,
            device_id=device,
            device_id_type=pl.DeviceIdType.MESH,
        )

    def begin(self, copy):
        copy.start()
        self.sending.append(copy)
        return copy

    def send_halo(self, kind):
        source, target, sign = self.halo[kind]
        depth, rows, width = source.shape
        border = rows // 8
        for direction, (delta_x, delta_y) in enumerate(OFFSETS):
            part = pl.ds(direction * border, border)
            goes = self.inside(sign * delta_x, sign * delta_y)
            comes = self.inside(-sign * delta_x, -sign * delta_y)
            copy = self.copy(
                source.at[:, part, :],
                target.at[:, part, :],
                self.halo_sems[0].at[kind, direction],
                self.halo_sems[1].at[kind, direction],
                self.offset(sign * delta_x, sign * delta_y),
            )

            @pl.when(goes)
            def _():
                copy.start()

            @pl.when(jnp.logical_not(comes))
            def _():
                target[:, part, :] = jnp.zeros((depth, border, width), BF16)

            self.exchanges.append((copy, goes, comes))

    def open(self, layer, layers):
        rows = self.grads.shape[0] // layers
        for number, (start, size) in enumerate(
            stream_ranges(rows, self.sizes[0] * self.sizes[1])
        ):
            stream = dict(
                slot=len(self.streams),
                order=self.orders[number],
                low=layer * rows + start,
                span=size,
                step=0,
                past=[],
            )
            self.streams.append(stream)
            self.reduce_start(stream)

    def block(self, start, size):
        return pl.ds(pl.multiple_of(start, 16), size)

    def reduce_start(self, stream):
        step, half = stream["step"], stream["span"] // 2
        where = stream["order"][step]
        bit = self.bit(where)
        stream["past"].append((stream["low"], stream["span"]))
        give = stream["low"] + (1 - bit) * half
        stream["target"] = self.landing.at[pl.ds(self.landed, half), :]
        stream["copy"] = self.begin(
            self.copy(
                self.work.at[self.block(give, half), :],
                stream["target"],
                self.sems[0].at[stream["slot"], step],
                self.sems[1].at[stream["slot"], step],
                self.partner(where),
            )
        )
        stream["low"], stream["span"] = stream["low"] + bit * half, half
        self.landed += half

    def gather_start(self, stream):
        step = stream["step"]
        where = stream["order"][2 * self.steps - 1 - step]
        here = self.block(stream["low"], stream["span"])
        stream["copy"] = self.begin(
            self.copy(
                self.sum.at[here, :],
                self.sum.at[here, :],
                self.sems[0].at[stream["slot"], step],
                self.sems[1].at[stream["slot"], step],
                self.partner(where),
            )
        )
        stream["low"], stream["span"] = stream["past"].pop()

    def advance_one(self, stream):
        stream["copy"].wait_recv()
        step = stream["step"]
        stream["step"] = step + 1
        if step < self.steps:
            here = self.block(stream["low"], stream["span"])
            total = self.grads[here, :] + stream["target"][...].astype(F32)
            if step + 1 < self.steps:
                self.grads[here, :] = total
                self.work[here, :] = total.astype(BF16)
                self.reduce_start(stream)
            else:
                self.sum[here, :] = total.astype(BF16)
                squares = jnp.sum((total * total).reshape(-1, 8, LANES), axis=0)
                self.squares = squares if self.squares is None else self.squares + squares
                self.gather_start(stream)
        elif step + 1 < 2 * self.steps:
            self.gather_start(stream)

    def advance(self):
        for stream in self.streams:
            if stream["step"] < 2 * self.steps:
                self.advance_one(stream)

    def small_start(self, small):
        step, kind = small["step"], small["kind"]
        acc, land = self.small[kind]
        small["copy"] = self.begin(
            self.copy(
                acc.at[step],
                land.at[step],
                self.small_sems[0].at[kind, step],
                self.small_sems[1].at[kind, step],
                self.partner(self.orders[0][step]),
            )
        )

    def open_small(self, kind):
        small = dict(kind=kind, step=0)
        self.small_start(small)
        return small

    def advance_small(self, small):
        step = small["step"]
        acc, land = self.small[small["kind"]]
        small["copy"].wait_recv()
        acc[step + 1] = acc[step] + land[step]
        small["step"] = step + 1
        if step + 1 < self.steps:
            self.small_start(small)

    def open_gate(self, gate_grad):
        acc = self.small[0][0]
        for row in range(acc.shape[1]):
            acc[0, row : row + 1, :] = gate_grad[:, row * LANES : (row + 1) * LANES]
        self.smalls.append(self.open_small(0))

    def finish(self):
        steps = self.steps
        while any(stream["step"] < 2 * steps for stream in self.streams) or any(
            small["step"] < steps for small in self.smalls
        ):
            self.advance()
            for small in self.smalls:
                if small["step"] < steps:
                    self.advance_small(small)
            if len(self.smalls) == 1 and all(stream["step"] >= steps for stream in self.streams):
                self.small[1][0][0] = self.squares
                self.smalls.append(self.open_small(1))
        for copy, goes, comes in self.exchanges:
            pl.when(comes)(copy.wait_recv)
            pl.when(goes)(copy.wait_send)
        for copy in self.sending:
            copy.wait_send()
        gate = self.small[0][0][steps]
        square = jnp.sum(self.small[1][0][steps], keepdims=True)
        return gate, square + jnp.sum(gate * gate, keepdims=True)


LOADED = (
    "nbr",
    "mask",
    "expr",
    "halo_expr",
    "cells",
    "halo",
    "self",
    "neigh",
    "stale_halo",
    "send",
    "cot",
    "stale_ret",
)


def step_kernel(sizes, *refs):
    total = len(LOADED)
    live_ref, lig_ref, rec_ref, gate_ref = refs[:4]
    far = refs[4 : 4 + total]
    fresh_ref, returned_ref, sum_ref, gate_out_ref, clip_ref = refs[4 + total : 9 + total]
    near = refs[9 + total : 9 + 2 * total]
    (
        count_ref,
        adj_t_ref,
        adj_low_ref,
        slope_ref,
        prod_ref,
        genes_ref,
        sent_ref,
        halo_grad_ref,
        grads_ref,
        sems,
    ) = refs[9 + 2 * total : 19 + 2 * total]
    link = Exchange(
        sizes,
        grads_ref,
        sum_ref,
        sent_ref,
        halo_grad_ref,
        fresh_ref,
        returned_ref,
        *refs[19 + 2 * total :],
    )
    link.announce()
    copies = {}
    for position, name in enumerate(LOADED):
        copies[name] = pltpu.make_async_copy(far[position], near[position], sems.at[position])
        copies[name].start()
    place = dict(zip(LOADED, near))

    def arrived(name):
        copies[name].wait()
        return place[name]

    layers = place["self"].shape[0]
    cells, width = place["cells"].shape[2:]
    halo = place["halo"].shape[2]
    joined_rows = cells + halo
    genes = place["expr"].shape[3]
    chunk = halo

    nbr_ref, mask_ref = arrived("nbr"), arrived("mask")
    count_edges(nbr_ref, mask_ref, count_ref)

    receptor_hot = one_hot(rec_ref[...], genes)
    ligand_hot = one_hot(lig_ref[...], genes).astype(BF16)
    gate_high, gate_low = split(gate_ref[...])
    zero = jnp.zeros((), BF16)
    mix = mm_nt(jnp.where(receptor_hot, gate_high, zero), ligand_hot)
    mix = mix + mm_nt(jnp.where(receptor_hot, gate_low, zero), ligand_hot)
    mix_high, mix_low = split(mix)
    expr = arrived("expr")[0, 0]
    scaled_high, scaled_low = split(mm(expr, mix_high) + mm(expr, mix_low))
    genes_ref[0:cells, :] = expr
    genes_ref[cells:, :] = arrived("halo_expr")[0, 0]

    def score_chunk(step, carry):
        rows = pl.ds(pl.multiple_of(step * chunk, chunk), chunk)
        here = genes_ref[rows, :]
        score = mm_nt(here, scaled_high) + mm_nt(here, scaled_low)
        gate = sigmoid(score)
        base = 0.25 * count_ref[rows, :].astype(F32) * gate
        high, low = split(base)
        adj_t_ref[rows, :] = high
        adj_low_ref[rows, :] = low
        slope_ref[rows, :] = base * (1.0 - gate)
        return carry

    lax.fori_loop(0, joined_rows // chunk, score_chunk, 0)

    adjacency = adj_t_ref[...].T
    adjacency_low = adj_low_ref[...].T
    state = arrived("cells")[0, 0]
    halo_ref, self_ref, neigh_ref = arrived("halo"), arrived("self"), arrived("neigh")
    stale_halo_ref = arrived("stale_halo")
    states, full_rows, aggregates, pre_acts = [], [], [], []
    for layer in range(layers):
        halo_rows = halo_ref[0, 0] if layer == 0 else stale_halo_ref[0, 0, layer - 1]
        joined = jnp.concatenate([state, halo_rows], 0)
        aggregate = (mm(adjacency, joined) + mm(adjacency_low, joined)).astype(BF16)
        pre_act = mm(state, self_ref[layer]) + mm(aggregate, neigh_ref[layer])
        states.append(state)
        full_rows.append(joined)
        aggregates.append(aggregate)
        pre_acts.append(pre_act)
        if layer + 1 < layers:
            state = (state.astype(F32) + pre_act * sigmoid(pre_act)).astype(BF16)

    send_table = one_hot(flat_rows(arrived("send")), cells).astype(BF16)
    for layer in range(1, layers):
        sent_ref[layer - 1] = mm_tn(send_table, states[layer]).astype(BF16)
    link.meet()
    link.send_halo(0)

    cot_ref, stale_ret_ref = arrived("cot"), arrived("stale_ret")
    live = lax.broadcasted_iota(jnp.int32, (cells, width), 0) < live_ref[0, 0]
    grad_state = jnp.where(live, cot_ref[0, 0].astype(F32), 0.0)
    grad_aggregates = [None] * layers
    for layer in range(layers - 1, -1, -1):
        grad_pre = (grad_state * silu_slope(pre_acts[layer])).astype(BF16)
        for position, left in enumerate((states[layer], aggregates[layer])):
            product = mm_tn(left, grad_pre)
            for lane in range(0, width, LANES):
                start = (2 * layer + position) * width * width // LANES + lane // LANES * width
                grads_ref[start : start + width, :] = product[:, lane : lane + LANES]
                link.work[start : start + width, :] = product[:, lane : lane + LANES].astype(BF16)
        link.open(layer, layers)
        grad_aggregate = mm_nt(grad_pre, neigh_ref[layer]).astype(BF16)
        grad_aggregates[layer] = grad_aggregate
        if layer > 0:
            grad_full = mm(adj_t_ref[...], grad_aggregate)
            halo_grad_ref[layer - 1] = grad_full[cells:].astype(BF16)
            grad_state = (
                grad_state
                + mm_nt(grad_pre, self_ref[layer])
                + grad_full[:cells]
                + mm(send_table, stale_ret_ref[0, 0, layer - 1])
            )
            link.advance()
    link.send_halo(1)

    for start in range(0, joined_rows, chunk):
        inner = jnp.zeros((chunk, cells), F32)
        for layer in range(layers):
            inner = inner + mm_nt(
                full_rows[layer][start : start + chunk], grad_aggregates[layer]
            )
        score_grad = (slope_ref[start : start + chunk, :] * inner).astype(BF16)
        prod_ref[start : start + chunk, :] = mm(score_grad, expr).astype(BF16)
        link.advance()
    pair_grads = mm_tn(genes_ref[...], prod_ref[...]).astype(BF16)
    link.advance()
    picked = mm(pair_grads, receptor_hot.astype(BF16))
    gate_grad = jnp.sum(picked * ligand_hot.astype(F32), axis=0, keepdims=True)
    link.open_gate(gate_grad)
    gate_sum, square = link.finish()
    clip = jnp.minimum(1.0, 2.0 * width / jnp.sqrt(square + 1e-06))
    clip_ref[...] = jnp.broadcast_to(clip, clip_ref.shape)
    gate_out_ref[...] = gate_sum


def run_step(sizes, *args):
    (
        cells,
        halo_inputs,
        stale_halo,
        stale_returned,
        cotangent,
        expression,
        halo_expression,
        neighbours,
        edge_mask,
        send_rows,
        live_cells,
        ligand_genes,
        receptor_genes,
        gate_weights,
        self_weights,
        neighbour_weights,
    ) = args
    layers, width, _ = self_weights.shape
    count, halo = cells.shape[2], halo_inputs.shape[2]
    genes, pairs = expression.shape[3], ligand_genes.shape[0]
    vmem = pl.BlockSpec(memory_space=pltpu.VMEM)
    smem = pl.BlockSpec(memory_space=pltpu.SMEM)
    hbm = pl.BlockSpec(memory_space=pltpu.HBM)
    named = dict(
        nbr=neighbours,
        mask=edge_mask,
        expr=expression,
        halo_expr=halo_expression,
        cells=cells,
        halo=halo_inputs,
        self=self_weights,
        neigh=neighbour_weights,
        stale_halo=stale_halo,
        send=send_rows,
        cot=cotangent,
        stale_ret=stale_returned,
    )
    loaded = [named[name] for name in LOADED]
    rows = 2 * layers * width * width // LANES
    steps = bits_of(sizes[0] * sizes[1])
    streams = layers * len(stream_ranges(rows // layers, sizes[0] * sizes[1]))
    edges = (layers - 1, halo, width)
    gate_tile = (pairs // LANES, LANES)
    return pl.pallas_call(
        functools.partial(step_kernel, sizes),
        out_shape=(
            jax.ShapeDtypeStruct(edges, BF16),
            jax.ShapeDtypeStruct(edges, BF16),
            jax.ShapeDtypeStruct((rows, LANES), BF16),
            jax.ShapeDtypeStruct(gate_tile, F32),
            jax.ShapeDtypeStruct((8, LANES), F32),
        ),
        in_specs=[smem] + [vmem] * 3 + [hbm] * len(loaded),
        out_specs=(vmem,) * 5,
        scratch_shapes=[pltpu.VMEM(value.shape, value.dtype) for value in loaded]
        + [
            pltpu.VMEM((count + halo, count), BF16),
            pltpu.VMEM((count + halo, count), BF16),
            pltpu.VMEM((count + halo, count), BF16),
            pltpu.VMEM((count + halo, count), F32),
            pltpu.VMEM((count + halo, genes), BF16),
            pltpu.VMEM((count + halo, genes), BF16),
            pltpu.VMEM(edges, BF16),
            pltpu.VMEM(edges, BF16),
            pltpu.VMEM((rows, LANES), F32),
            pltpu.SemaphoreType.DMA((len(loaded),)),
            pltpu.VMEM((rows, LANES), BF16),
            pltpu.VMEM((rows, LANES), BF16),
            pltpu.VMEM((steps + 1,) + gate_tile, F32),
            pltpu.VMEM((steps + 1,) + gate_tile, F32),
            pltpu.VMEM((steps + 1, 8, LANES), F32),
            pltpu.VMEM((steps + 1, 8, LANES), F32),
            pltpu.SemaphoreType.DMA((streams, 2 * steps)),
            pltpu.SemaphoreType.DMA((streams, 2 * steps)),
            pltpu.SemaphoreType.DMA((2, steps)),
            pltpu.SemaphoreType.DMA((2, steps)),
            pltpu.SemaphoreType.DMA((2, 8)),
            pltpu.SemaphoreType.DMA((2, 8)),
        ],
        compiler_params=pltpu.CompilerParams(
            collective_id=0, has_side_effects=True, vmem_limit_bytes=58 * 1024 * 1024
        ),
        name="step",
    )(
        live_cells,
        ligand_genes.reshape(1, -1),
        receptor_genes.reshape(1, -1),
        gate_weights.reshape(1, -1),
        *loaded,
    )


def finish_kernel(
    fresh_ref,
    returned_ref,
    sum_ref,
    clip_ref,
    gate_ref,
    fresh_out,
    returned_out,
    layer_out,
    gate_out,
    sum_near,
    layer_near,
    pass_sems,
    load_sems,
    store_sems,
):
    count, width, _ = layer_near.shape
    span = width * width // LANES
    passes = []
    for position, (source, target) in enumerate(
        ((fresh_ref, fresh_out), (returned_ref, returned_out))
    ):
        passes.append(
            pltpu.make_async_copy(source, target.at[0, 0], pass_sems.at[position])
        )
    loads = [
        pltpu.make_async_copy(
            sum_ref.at[pl.ds(index * span, span), :],
            sum_near.at[pl.ds(index * span, span), :],
            load_sems.at[index],
        )
        for index in range(count)
    ]
    stores = [
        pltpu.make_async_copy(layer_near.at[index], layer_out.at[index], store_sems.at[index])
        for index in range(count)
    ]
    for copy in loads + passes:
        copy.start()
    clip = clip_ref[0:1, 0:1]
    gate_out[...] = gate_ref[...] * clip
    for index in range(count):
        loads[index].wait()
        for lane in range(0, width, LANES):
            start = index * span + lane // LANES * width
            part = sum_near[start : start + width, :].astype(F32)
            layer_near[index, :, lane : lane + LANES] = part * clip
        stores[index].start()
    for copy in stores + passes:
        copy.wait()


def finish(layers, width, fresh, returned, layer_sum, clip, gate):
    hbm = pl.BlockSpec(memory_space=pltpu.HBM)
    vmem = pl.BlockSpec(memory_space=pltpu.VMEM)
    count = 2 * layers
    return pl.pallas_call(
        finish_kernel,
        out_shape=(
            jax.ShapeDtypeStruct((1, 1) + fresh.shape, BF16),
            jax.ShapeDtypeStruct((1, 1) + fresh.shape, BF16),
            jax.ShapeDtypeStruct((count, width, width), F32),
            jax.ShapeDtypeStruct(gate.shape, F32),
        ),
        in_specs=[hbm, hbm, hbm, vmem, vmem],
        out_specs=(hbm, hbm, hbm, vmem),
        scratch_shapes=[
            pltpu.VMEM(layer_sum.shape, BF16),
            pltpu.VMEM((count, width, width), F32),
            pltpu.SemaphoreType.DMA((2,)),
            pltpu.SemaphoreType.DMA((count,)),
            pltpu.SemaphoreType.DMA((count,)),
        ],
        compiler_params=pltpu.CompilerParams(vmem_limit_bytes=58 * 1024 * 1024),
        name="finish",
    )(fresh, returned, layer_sum, clip, gate)


def on_device(sizes, *args):
    self_weights = args[14]
    layers, width, _ = self_weights.shape
    fresh, returned, layer_sum, gate, clip = run_step(sizes, *args)
    fresh, returned, layer_part, gate = finish(
        layers, width, fresh, returned, layer_sum, clip, gate
    )
    return fresh, returned, layer_part, gate.reshape(-1)


def solution(mesh):
    tile = P("tx", "ty")
    sizes = (mesh.shape["tx"], mesh.shape["ty"])
    return jax.shard_map(
        functools.partial(on_device, sizes),
        mesh=mesh,
        in_specs=(tile,) * 11 + (P(),) * 5,
        out_specs=(tile, tile, P(), P()),
        check_vma=False,
    )
```

```python
import functools

import jax
import jax.numpy as jnp
from jax import lax
from jax.experimental import pallas as pl
from jax.experimental.pallas import tpu as pltpu
from jax.sharding import PartitionSpec as P

OFFSETS = ((-1, -1), (-1, 0), (-1, 1), (0, -1), (0, 1), (1, -1), (1, 0), (1, 1))
F32 = jnp.float32
BF16 = jnp.bfloat16
LANES = 128


def mm(a, b):
    return jnp.dot(a, b, preferred_element_type=F32)


def mm_nt(a, b):
    return lax.dot_general(a, b, (((1,), (1,)), ((), ())), preferred_element_type=F32)


def mm_tn(a, b):
    return lax.dot_general(a, b, (((0,), (0,)), ((), ())), preferred_element_type=F32)


def split(value):
    high = value.astype(BF16)
    return high, (value - high.astype(F32)).astype(BF16)


def sigmoid(value):
    return jax.nn.sigmoid(value)


def silu_slope(pre_act):
    gate = sigmoid(pre_act)
    return gate * (1.0 + pre_act * (1.0 - gate))


def count_edges(nbr_ref, mask_ref, count_ref):
    degree, cells = nbr_ref.shape[2:]
    rows = count_ref.shape[0]
    step, group = 64, 256
    for lane in range(0, cells, 128):
        for first in range(0, rows, group):
            ids = []
            for k in range(degree):
                here = nbr_ref[0, 0, k : k + 1, lane : lane + 128] - first
                real = mask_ref[0, 0, k : k + 1, lane : lane + 128]
                near = jnp.where(real > 0, here, -1).astype(F32)
                ids.append(jnp.broadcast_to(near, (16, 128)).astype(BF16))

            def body(chunk, carry):
                for part in range(0, step, 16):
                    base = chunk * step + part
                    row = lax.broadcasted_iota(jnp.int32, (16, 128), 0) + base
                    row = row.astype(F32).astype(BF16)
                    total = jnp.zeros((16, 128), BF16)
                    one = jnp.ones((16, 128), BF16)
                    for k in range(degree):
                        total = total + jnp.where(ids[k] == row, one, jnp.zeros_like(one))
                    start = pl.multiple_of(first + base, 16)
                    count_ref[pl.ds(start, 16), lane : lane + 128] = total
                return carry

            lax.fori_loop(0, min(group, rows - first) // step, body, 0)


def one_hot(ids, rows):
    return lax.broadcasted_iota(jnp.int32, (rows, ids.shape[1]), 0) == ids


def flat_rows(send_ref):
    directions, border = send_ref.shape[2:]
    total = directions * border
    ids = send_ref[0, 0]
    spread = (
        lax.broadcasted_iota(jnp.int32, (border, total), 1) % border
        == lax.broadcasted_iota(jnp.int32, (border, total), 0)
    ).astype(BF16)
    high = mm((ids // 256).astype(F32).astype(BF16), spread)
    low = mm((ids % 256).astype(F32).astype(BF16), spread)
    wide = high * 256.0 + low
    mine = lax.broadcasted_iota(
        jnp.int32, (directions, total), 1
    ) // border == lax.broadcasted_iota(jnp.int32, (directions, total), 0)
    return jnp.sum(jnp.where(mine, wide, 0.0), axis=0, keepdims=True).astype(jnp.int32)


def bits_of(size):
    assert size & (size - 1) == 0
    return size.bit_length() - 1


def stream_orders(tx_size, ty_size):
    tx_bits = [("tx", bit) for bit in range(bits_of(tx_size))]
    ty_bits = [("ty", bit) for bit in range(bits_of(ty_size))]

    def paired(bits):
        return [tuple(bits[at : at + 2]) for at in range(0, len(bits), 2)]

    first, near, far = paired(tx_bits[:1]), paired(ty_bits + tx_bits[1:2]), paired(tx_bits[2:])
    return (first + near + far, first + near + far, first + far + near)


def messages_of(order):
    return sum((1 << len(stage)) - 1 for stage in order)


def stream_ranges(rows, devices):
    unit = 16 * devices
    units = rows // unit
    assert units * unit == rows and units > 0
    used = min(3, units)
    ranges, start = [], 0
    for stream in range(used):
        size = (units // used + (1 if stream < units % used else 0)) * unit
        ranges.append((start, size))
        start += size
    return ranges


class Exchange:
    def __init__(
        self,
        sizes,
        grads_ref,
        sum_ref,
        sent_ref,
        halo_grad_ref,
        fresh_ref,
        returned_ref,
        work_ref,
        landing_ref,
        gate_acc,
        gate_land,
        square_acc,
        square_land,
        send_sems,
        recv_sems,
        small_send,
        small_recv,
        halo_send,
        halo_recv,
    ):
        self.sizes = sizes
        self.me = {"tx": lax.axis_index("tx"), "ty": lax.axis_index("ty")}
        self.grads, self.sum, self.work, self.landing = grads_ref, sum_ref, work_ref, landing_ref
        self.halo = ((sent_ref, fresh_ref, 1), (halo_grad_ref, returned_ref, -1))
        self.small = ((gate_acc, gate_land), (square_acc, square_land))
        self.sems = (send_sems, recv_sems)
        self.small_sems = (small_send, small_recv)
        self.halo_sems = (halo_send, halo_recv)
        self.orders = stream_orders(*sizes)
        self.steps = len(self.orders[0])
        self.landed = 0
        self.streams = []
        self.smalls = []
        self.sending = []
        self.exchanges = []
        self.squares = None

    def bit(self, where):
        axis, bit = where
        return (self.me[axis] // (1 << bit)) % 2

    def partner(self, stage, flips):
        place = dict(self.me)
        for position, where in enumerate(stage):
            if flips >> position & 1:
                place[where[0]] = place[where[0]] + (1 - 2 * self.bit(where)) * (1 << where[1])
        return place

    def digit(self, stage, flips):
        total = 0
        for position, where in enumerate(stage):
            bit = self.bit(where)
            total = total + ((1 - bit) if flips >> position & 1 else bit) * (1 << position)
        return total

    def inside(self, delta_x, delta_y):
        x, y = self.me["tx"] + delta_x, self.me["ty"] + delta_y
        return (x >= 0) & (x < self.sizes[0]) & (y >= 0) & (y < self.sizes[1])

    def offset(self, delta_x, delta_y):
        return {"tx": self.me["tx"] + delta_x, "ty": self.me["ty"] + delta_y}

    def announce(self):
        barrier = pltpu.get_barrier_semaphore()

        def greet(device):
            pl.semaphore_signal(
                barrier, inc=1, device_id=device, device_id_type=pl.DeviceIdType.MESH
            )

        for stage in self.orders[0]:
            for flips in range(1, 1 << len(stage)):
                greet(self.partner(stage, flips))
        for offset in OFFSETS:
            pl.when(self.inside(*offset))(lambda offset=offset: greet(self.offset(*offset)))

    def meet(self):
        barrier = pltpu.get_barrier_semaphore()
        peers = messages_of(self.orders[0])
        for offset in OFFSETS:
            peers = peers + self.inside(*offset).astype(jnp.int32)
        pl.semaphore_wait(barrier, peers)

    def copy(self, source, target, send, recv, device):
        return pltpu.make_async_remote_copy(
            src_ref=source,
            dst_ref=target,
            send_sem=send,
            recv_sem=recv,
            device_id=device,
            device_id_type=pl.DeviceIdType.MESH,
        )

    def begin(self, copy):
        copy.start()
        self.sending.append(copy)
        return copy

    def send_halo(self, kind):
        source, target, sign = self.halo[kind]
        depth, rows, width = source.shape
        border = rows // 8
        for direction, (delta_x, delta_y) in enumerate(OFFSETS):
            part = pl.ds(direction * border, border)
            goes = self.inside(sign * delta_x, sign * delta_y)
            comes = self.inside(-sign * delta_x, -sign * delta_y)
            copy = self.copy(
                source.at[:, part, :],
                target.at[:, part, :],
                self.halo_sems[0].at[kind, direction],
                self.halo_sems[1].at[kind, direction],
                self.offset(sign * delta_x, sign * delta_y),
            )

            @pl.when(goes)
            def _():
                copy.start()

            @pl.when(jnp.logical_not(comes))
            def _():
                target[:, part, :] = jnp.zeros((depth, border, width), BF16)

            self.exchanges.append((copy, goes, comes))

    def open(self, layer, layers):
        rows = self.grads.shape[0] // layers
        for number, (start, size) in enumerate(
            stream_ranges(rows, self.sizes[0] * self.sizes[1])
        ):
            stream = dict(
                slot=len(self.streams),
                layer=layer,
                order=self.orders[number],
                low=layer * rows + start,
                span=size,
                step=0,
                sent=0,
                past=[],
            )
            self.streams.append(stream)
            self.reduce_start(stream)

    def block(self, start, size):
        return pl.ds(pl.multiple_of(start, 16), size)

    def send_part(self, stream, source, target, stage, flips):
        number = stream["sent"]
        stream["sent"] = number + 1
        return self.begin(
            self.copy(
                source,
                target,
                self.sems[0].at[stream["slot"], number],
                self.sems[1].at[stream["slot"], number],
                self.partner(stage, flips),
            )
        )

    def reduce_start(self, stream):
        stage = stream["order"][stream["step"]]
        radix = 1 << len(stage)
        piece = stream["span"] // radix
        stream["past"].append((stream["low"], stream["span"]))
        stream["copies"], stream["targets"] = [], []
        for flips in range(1, radix):
            give = stream["low"] + self.digit(stage, flips) * piece
            target = self.landing.at[pl.ds(self.landed, piece), :]
            source = self.work.at[self.block(give, piece), :]
            stream["copies"].append(self.send_part(stream, source, target, stage, flips))
            stream["targets"].append(target)
            self.landed += piece
        stream["low"] = stream["low"] + self.digit(stage, 0) * piece
        stream["span"] = piece

    def gather_start(self, stream):
        stage = stream["order"][2 * self.steps - 1 - stream["step"]]
        here = self.sum.at[self.block(stream["low"], stream["span"]), :]
        stream["copies"] = [
            self.send_part(stream, here, here, stage, flips)
            for flips in range(1, 1 << len(stage))
        ]
        stream["low"], stream["span"] = stream["past"].pop()

    def advance_one(self, stream):
        for copy in stream["copies"]:
            copy.wait_recv()
        step = stream["step"]
        stream["step"] = step + 1
        if step < self.steps:
            here = self.block(stream["low"], stream["span"])
            total = self.grads[here, :]
            for target in stream["targets"]:
                total = total + target[...].astype(F32)
            if step + 1 < self.steps:
                self.grads[here, :] = total
                self.work[here, :] = total.astype(BF16)
                self.reduce_start(stream)
            else:
                self.sum[here, :] = total.astype(BF16)
                squares = jnp.sum((total * total).reshape(-1, 8, LANES), axis=0)
                self.squares = squares if self.squares is None else self.squares + squares
                self.gather_start(stream)
        elif step + 1 < 2 * self.steps:
            self.gather_start(stream)

    def advance(self, layer=None):
        for stream in self.streams:
            if stream["step"] < 2 * self.steps and layer in (None, stream["layer"]):
                self.advance_one(stream)

    def small_start(self, small):
        step, kind = small["step"], small["kind"]
        acc, land = self.small[kind]
        stage = self.orders[0][step]
        first = messages_of(self.orders[0][:step])
        small["slots"], small["copies"] = [], []
        for flips in range(1, 1 << len(stage)):
            slot = first + flips - 1
            copy = self.copy(
                acc.at[step],
                land.at[slot],
                self.small_sems[0].at[kind, slot],
                self.small_sems[1].at[kind, slot],
                self.partner(stage, flips),
            )
            small["copies"].append(self.begin(copy))
            small["slots"].append(slot)

    def open_small(self, kind):
        small = dict(kind=kind, step=0)
        self.small_start(small)
        return small

    def advance_small(self, small):
        step = small["step"]
        acc, land = self.small[small["kind"]]
        for copy in small["copies"]:
            copy.wait_recv()
        terms = [acc[step]] + [land[slot] for slot in small["slots"]]
        while len(terms) > 1:
            terms = [terms[at] + terms[at + 1] for at in range(0, len(terms), 2)]
        acc[step + 1] = terms[0]
        small["step"] = step + 1
        if step + 1 < self.steps:
            self.small_start(small)

    def open_gate(self, gate_grad):
        acc = self.small[0][0]
        for row in range(acc.shape[1]):
            acc[0, row : row + 1, :] = gate_grad[:, row * LANES : (row + 1) * LANES]
        self.smalls.append(self.open_small(0))

    def finish(self):
        steps = self.steps
        while any(stream["step"] < 2 * steps for stream in self.streams) or any(
            small["step"] < steps for small in self.smalls
        ):
            self.advance()
            for small in self.smalls:
                if small["step"] < steps:
                    self.advance_small(small)
            if len(self.smalls) == 1 and all(stream["step"] >= steps for stream in self.streams):
                self.small[1][0][0] = self.squares
                self.smalls.append(self.open_small(1))
        for copy, goes, comes in self.exchanges:
            pl.when(comes)(copy.wait_recv)
            pl.when(goes)(copy.wait_send)
        for copy in self.sending:
            copy.wait_send()
        gate = self.small[0][0][steps]
        square = jnp.sum(self.small[1][0][steps], keepdims=True)
        return gate, square + jnp.sum(gate * gate, keepdims=True)


LOADED = (
    "nbr",
    "mask",
    "expr",
    "halo_expr",
    "cells",
    "halo",
    "self",
    "neigh",
    "stale_halo",
    "send",
    "cot",
    "stale_ret",
)


def step_kernel(sizes, *refs):
    total = len(LOADED)
    live_ref, lig_ref, rec_ref, gate_ref = refs[:4]
    far = refs[4 : 4 + total]
    fresh_ref, returned_ref, sum_ref, gate_out_ref, clip_ref = refs[4 + total : 9 + total]
    near = refs[9 + total : 9 + 2 * total]
    (
        count_ref,
        adj_t_ref,
        adj_low_ref,
        slope_ref,
        prod_ref,
        genes_ref,
        sent_ref,
        halo_grad_ref,
        grads_ref,
        sems,
    ) = refs[9 + 2 * total : 19 + 2 * total]
    link = Exchange(
        sizes,
        grads_ref,
        sum_ref,
        sent_ref,
        halo_grad_ref,
        fresh_ref,
        returned_ref,
        *refs[19 + 2 * total :],
    )
    link.announce()
    copies = {}
    for position, name in enumerate(LOADED):
        copies[name] = pltpu.make_async_copy(far[position], near[position], sems.at[position])
        copies[name].start()
    place = dict(zip(LOADED, near))

    def arrived(name):
        copies[name].wait()
        return place[name]

    layers = place["self"].shape[0]
    cells, width = place["cells"].shape[2:]
    halo = place["halo"].shape[2]
    joined_rows = cells + halo
    genes = place["expr"].shape[3]
    chunk = halo

    nbr_ref, mask_ref = arrived("nbr"), arrived("mask")
    count_edges(nbr_ref, mask_ref, count_ref)

    receptor_hot = one_hot(rec_ref[...], genes)
    ligand_hot = one_hot(lig_ref[...], genes).astype(BF16)
    gate_high, gate_low = split(gate_ref[...])
    zero = jnp.zeros((), BF16)
    mix = mm_nt(jnp.where(receptor_hot, gate_high, zero), ligand_hot)
    mix = mix + mm_nt(jnp.where(receptor_hot, gate_low, zero), ligand_hot)
    mix_high, mix_low = split(mix)
    expr = arrived("expr")[0, 0]
    scaled_high, scaled_low = split(mm(expr, mix_high) + mm(expr, mix_low))
    genes_ref[0:cells, :] = expr
    genes_ref[cells:, :] = arrived("halo_expr")[0, 0]

    def score_chunk(step, carry):
        rows = pl.ds(pl.multiple_of(step * chunk, chunk), chunk)
        here = genes_ref[rows, :]
        score = mm_nt(here, scaled_high) + mm_nt(here, scaled_low)
        gate = sigmoid(score)
        base = 0.25 * count_ref[rows, :].astype(F32) * gate
        high, low = split(base)
        adj_t_ref[rows, :] = high
        adj_low_ref[rows, :] = low
        slope_ref[rows, :] = base * (1.0 - gate)
        return carry

    lax.fori_loop(0, joined_rows // chunk, score_chunk, 0)

    adjacency = adj_t_ref[...].T
    adjacency_low = adj_low_ref[...].T
    state = arrived("cells")[0, 0]
    halo_ref, self_ref, neigh_ref = arrived("halo"), arrived("self"), arrived("neigh")
    stale_halo_ref = arrived("stale_halo")
    states, full_rows, aggregates, pre_acts = [], [], [], []
    for layer in range(layers):
        halo_rows = halo_ref[0, 0] if layer == 0 else stale_halo_ref[0, 0, layer - 1]
        joined = jnp.concatenate([state, halo_rows], 0)
        aggregate = (mm(adjacency, joined) + mm(adjacency_low, joined)).astype(BF16)
        pre_act = mm(state, self_ref[layer]) + mm(aggregate, neigh_ref[layer])
        states.append(state)
        full_rows.append(joined)
        aggregates.append(aggregate)
        pre_acts.append(pre_act)
        if layer + 1 < layers:
            state = (state.astype(F32) + pre_act * sigmoid(pre_act)).astype(BF16)

    send_table = one_hot(flat_rows(arrived("send")), cells).astype(BF16)
    for layer in range(1, layers):
        sent_ref[layer - 1] = mm_tn(send_table, states[layer]).astype(BF16)
    link.meet()
    link.send_halo(0)

    cot_ref, stale_ret_ref = arrived("cot"), arrived("stale_ret")
    live = lax.broadcasted_iota(jnp.int32, (cells, width), 0) < live_ref[0, 0]
    grad_state = jnp.where(live, cot_ref[0, 0].astype(F32), 0.0)
    grad_aggregates = [None] * layers
    for layer in range(layers - 1, -1, -1):
        grad_pre = (grad_state * silu_slope(pre_acts[layer])).astype(BF16)
        for position, left in enumerate((states[layer], aggregates[layer])):
            product = mm_tn(left, grad_pre)
            for lane in range(0, width, LANES):
                start = (2 * layer + position) * width * width // LANES + lane // LANES * width
                grads_ref[start : start + width, :] = product[:, lane : lane + LANES]
                link.work[start : start + width, :] = product[:, lane : lane + LANES].astype(BF16)
        link.open(layer, layers)
        grad_aggregate = mm_nt(grad_pre, neigh_ref[layer]).astype(BF16)
        grad_aggregates[layer] = grad_aggregate
        if layer > 0:
            grad_full = mm(adj_t_ref[...], grad_aggregate)
            halo_grad_ref[layer - 1] = grad_full[cells:].astype(BF16)
            grad_state = (
                grad_state
                + mm_nt(grad_pre, self_ref[layer])
                + grad_full[:cells]
                + mm(send_table, stale_ret_ref[0, 0, layer - 1])
            )
            link.advance(layer)
    link.send_halo(1)

    for start in range(0, joined_rows, chunk):
        inner = jnp.zeros((chunk, cells), F32)
        for layer in range(layers):
            inner = inner + mm_nt(
                full_rows[layer][start : start + chunk], grad_aggregates[layer]
            )
        score_grad = (slope_ref[start : start + chunk, :] * inner).astype(BF16)
        prod_ref[start : start + chunk, :] = mm(score_grad, expr).astype(BF16)
        if start < layers * chunk:
            link.advance(start // chunk)
    pair_grads = mm_tn(genes_ref[...], prod_ref[...]).astype(BF16)
    picked = mm(pair_grads, receptor_hot.astype(BF16))
    gate_grad = jnp.sum(picked * ligand_hot.astype(F32), axis=0, keepdims=True)
    link.open_gate(gate_grad)
    gate_sum, square = link.finish()
    clip = jnp.minimum(1.0, 2.0 * width / jnp.sqrt(square + 1e-06))
    clip_ref[...] = jnp.broadcast_to(clip, clip_ref.shape)
    gate_out_ref[...] = gate_sum


def run_step(sizes, *args):
    (
        cells,
        halo_inputs,
        stale_halo,
        stale_returned,
        cotangent,
        expression,
        halo_expression,
        neighbours,
        edge_mask,
        send_rows,
        live_cells,
        ligand_genes,
        receptor_genes,
        gate_weights,
        self_weights,
        neighbour_weights,
    ) = args
    layers, width, _ = self_weights.shape
    count, halo = cells.shape[2], halo_inputs.shape[2]
    genes, pairs = expression.shape[3], ligand_genes.shape[0]
    vmem = pl.BlockSpec(memory_space=pltpu.VMEM)
    smem = pl.BlockSpec(memory_space=pltpu.SMEM)
    hbm = pl.BlockSpec(memory_space=pltpu.HBM)
    named = dict(
        nbr=neighbours,
        mask=edge_mask,
        expr=expression,
        halo_expr=halo_expression,
        cells=cells,
        halo=halo_inputs,
        self=self_weights,
        neigh=neighbour_weights,
        stale_halo=stale_halo,
        send=send_rows,
        cot=cotangent,
        stale_ret=stale_returned,
    )
    loaded = [named[name] for name in LOADED]
    rows = 2 * layers * width * width // LANES
    order = stream_orders(*sizes)[0]
    steps, messages = len(order), messages_of(order)
    streams = layers * len(stream_ranges(rows // layers, sizes[0] * sizes[1]))
    edges = (layers - 1, halo, width)
    gate_tile = (pairs // LANES, LANES)
    return pl.pallas_call(
        functools.partial(step_kernel, sizes),
        out_shape=(
            jax.ShapeDtypeStruct(edges, BF16),
            jax.ShapeDtypeStruct(edges, BF16),
            jax.ShapeDtypeStruct((rows, LANES), BF16),
            jax.ShapeDtypeStruct(gate_tile, F32),
            jax.ShapeDtypeStruct((8, LANES), F32),
        ),
        in_specs=[smem] + [vmem] * 3 + [hbm] * len(loaded),
        out_specs=(vmem,) * 5,
        scratch_shapes=[pltpu.VMEM(value.shape, value.dtype) for value in loaded]
        + [
            pltpu.VMEM((count + halo, count), BF16),
            pltpu.VMEM((count + halo, count), BF16),
            pltpu.VMEM((count + halo, count), BF16),
            pltpu.VMEM((count + halo, count), F32),
            pltpu.VMEM((count + halo, genes), BF16),
            pltpu.VMEM((count + halo, genes), BF16),
            pltpu.VMEM(edges, BF16),
            pltpu.VMEM(edges, BF16),
            pltpu.VMEM((rows, LANES), F32),
            pltpu.SemaphoreType.DMA((len(loaded),)),
            pltpu.VMEM((rows, LANES), BF16),
            pltpu.VMEM((rows, LANES), BF16),
            pltpu.VMEM((steps + 1,) + gate_tile, F32),
            pltpu.VMEM((messages,) + gate_tile, F32),
            pltpu.VMEM((steps + 1, 8, LANES), F32),
            pltpu.VMEM((messages, 8, LANES), F32),
            pltpu.SemaphoreType.DMA((streams, 2 * messages)),
            pltpu.SemaphoreType.DMA((streams, 2 * messages)),
            pltpu.SemaphoreType.DMA((2, messages)),
            pltpu.SemaphoreType.DMA((2, messages)),
            pltpu.SemaphoreType.DMA((2, 8)),
            pltpu.SemaphoreType.DMA((2, 8)),
        ],
        compiler_params=pltpu.CompilerParams(
            collective_id=0, has_side_effects=True, vmem_limit_bytes=58 * 1024 * 1024
        ),
        name="step",
    )(
        live_cells,
        ligand_genes.reshape(1, -1),
        receptor_genes.reshape(1, -1),
        gate_weights.reshape(1, -1),
        *loaded,
    )


def finish_kernel(
    fresh_ref,
    returned_ref,
    sum_ref,
    clip_ref,
    gate_ref,
    fresh_out,
    returned_out,
    layer_out,
    gate_out,
    sum_near,
    layer_near,
    halo_near,
    pass_sems,
    load_sems,
    store_sems,
):
    count, width, _ = layer_near.shape
    span = width * width // LANES
    halos = ((fresh_ref, fresh_out), (returned_ref, returned_out))
    into = [
        pltpu.make_async_copy(source, halo_near.at[position], pass_sems.at[0, position])
        for position, (source, _) in enumerate(halos)
    ]
    onward = [
        pltpu.make_async_copy(halo_near.at[position], target.at[0, 0], pass_sems.at[1, position])
        for position, (_, target) in enumerate(halos)
    ]
    loads = [
        pltpu.make_async_copy(
            sum_ref.at[pl.ds(index * span, span), :],
            sum_near.at[pl.ds(index * span, span), :],
            load_sems.at[index],
        )
        for index in range(count)
    ]
    stores = [
        pltpu.make_async_copy(layer_near.at[index], layer_out.at[index], store_sems.at[index])
        for index in range(count)
    ]
    for copy in loads + into:
        copy.start()
    clip = clip_ref[0:1, 0:1]
    gate_out[...] = gate_ref[...] * clip
    for index in range(count):
        loads[index].wait()
        for lane in range(0, width, LANES):
            start = index * span + lane // LANES * width
            part = sum_near[start : start + width, :].astype(F32)
            layer_near[index, :, lane : lane + LANES] = part * clip
        stores[index].start()
    for position in range(len(halos)):
        into[position].wait()
        onward[position].start()
    for copy in stores + onward:
        copy.wait()


def finish(layers, width, fresh, returned, layer_sum, clip, gate):
    hbm = pl.BlockSpec(memory_space=pltpu.HBM)
    vmem = pl.BlockSpec(memory_space=pltpu.VMEM)
    count = 2 * layers
    return pl.pallas_call(
        finish_kernel,
        out_shape=(
            jax.ShapeDtypeStruct((1, 1) + fresh.shape, BF16),
            jax.ShapeDtypeStruct((1, 1) + fresh.shape, BF16),
            jax.ShapeDtypeStruct((count, width, width), F32),
            jax.ShapeDtypeStruct(gate.shape, F32),
        ),
        in_specs=[hbm, hbm, hbm, vmem, vmem],
        out_specs=(hbm, hbm, hbm, vmem),
        scratch_shapes=[
            pltpu.VMEM(layer_sum.shape, BF16),
            pltpu.VMEM((count, width, width), F32),
            pltpu.VMEM((2,) + fresh.shape, BF16),
            pltpu.SemaphoreType.DMA((2, 2)),
            pltpu.SemaphoreType.DMA((count,)),
            pltpu.SemaphoreType.DMA((count,)),
        ],
        compiler_params=pltpu.CompilerParams(vmem_limit_bytes=58 * 1024 * 1024),
        name="finish",
    )(fresh, returned, layer_sum, clip, gate)


def on_device(sizes, *args):
    self_weights = args[14]
    layers, width, _ = self_weights.shape
    fresh, returned, layer_sum, gate, clip = run_step(sizes, *args)
    fresh, returned, layer_part, gate = finish(
        layers, width, fresh, returned, layer_sum, clip, gate
    )
    return fresh, returned, layer_part, gate.reshape(-1)


def solution(mesh):
    tile = P("tx", "ty")
    sizes = (mesh.shape["tx"], mesh.shape["ty"])
    return jax.shard_map(
        functools.partial(on_device, sizes),
        mesh=mesh,
        in_specs=(tile,) * 11 + (P(),) * 5,
        out_specs=(tile, tile, P(), P()),
        check_vma=False,
    )
```
